1024 devices in a mesh: row: 8 (over y, core), col: 128 (over z, x).
Axes of the slice: x: 4, y: 4, z: 32, core: 2. Of those that a mesh axis runs over, the one named last changes fastest.
Arguments:
- conc: float32 [118784, 512], P(('row', 'col')), may hold values from -1 to 1
- levels: int32 [118784], P(('row', 'col')), may hold values from 0 to 2
- neighbours: int32 [6, 118784], P(None, ('row', 'col')), may hold values from -1 to 98303, as said below
- hanging: int32 [6, 118784], P(None, ('row', 'col')), may hold values 0 or 1
- block_counts: int32 [1024], replicated, may hold values from 76 to 116, as said below
Outputs:
- conc_next: float32 [118784, 512], P(('row', 'col'))
- potential: float32 [118784, 512], P(('row', 'col'))
The draws below stay inside these ranges and needn't reach their ends.
Inputs may be any that keep to these rules, and one draw needn't show every extreme that they name: `neighbours`: slots at or past a device's count hold -1. A live block's faces name live blocks, matched: if block a's face f names b, then b's face f xor 1 names a. A named block lies on the same device, on another device of the same row, or on the device of the same col in the row before or after (rows taken periodically). Between two devices of one row, in each direction, either no face or exactly 2 faces cross. Between a device and the device of the same col in the next row, 1 to 16 matched face pairs come in each direction's pair count, so 2 to 32 faces cross each way, 32 in some pairs of every draw. `block_counts`: the counts sum to 98304; the largest is 116.
All inputs are finite; a program needn't handle non-finite values. No bound on the sum of `hanging` on one device may be relied on, other than what follows from the above.
Results may differ from the reference program's by a relative error of at most 0.00005.
Values sent between devices are 32-bit elements; how exact they have to be, the bound alone decides.
A program may use at most 32 MiB of HBM per device.

```python
import jax
import jax.numpy as jnp
from jax import lax

AVG = 96
KMAX = 16
MINB = 76
CAP = 116
SLOT_TOTAL_COUNT = 118784
N_ROW = 8
N_COL = 128
DEVICES = 1024


def rewire(owners, slot_ids, counts, first_dev, first_pos, second_dev, second_pos, direction, active):
    stride = (1, 5, 17)[direction]
    plane = N_ROW * N_COL * CAP
    first_next = (first_pos + stride) % counts[first_dev]
    second_next = (second_pos + stride) % counts[second_dev]
    lower_face = 2 * direction * plane
    upper_face = (2 * direction + 1) * plane
    where_to = jnp.concatenate([upper_face + first_dev * CAP + first_pos, lower_face + second_dev * CAP + second_next, upper_face + second_dev * CAP + second_pos, lower_face + first_dev * CAP + first_next])
    owner_new = jnp.concatenate([second_dev, first_dev, first_dev, second_dev])
    slot_new = jnp.concatenate([second_next, first_pos, first_next, second_pos])
    selected_entries = jnp.concatenate([active, active, active, active])
    where_to = jnp.where(selected_entries, where_to, 6 * plane).astype(jnp.int32)
    owners = owners.at[where_to].set(owner_new.astype(jnp.int32), mode='drop')
    slot_ids = slot_ids.at[where_to].set(slot_new.astype(jnp.int32), mode='drop')
    return (owners, slot_ids)


def forest_layout(key):
    devices = N_ROW * N_COL
    half = N_COL // 2
    key_counts = jax.random.fold_in(key, 101)
    key_far = jax.random.fold_in(key, 102)
    key_slab = jax.random.fold_in(key, 103)
    leading = jax.random.randint(key_counts, (devices // 2,), MINB, CAP + 1).astype(jnp.int32)
    leading = leading.at[0].set(CAP)
    counts = jnp.stack([leading, 2 * AVG - leading], axis=1).reshape(devices).astype(jnp.int32)
    offsets = (jnp.cumsum(counts) - counts).astype(jnp.int32)
    device = jnp.arange(devices, dtype=jnp.int32)
    within = jnp.arange(CAP, dtype=jnp.int32)
    row_of = device // N_COL
    col_of = device % N_COL
    owner_parts = []
    slot_parts = []
    for direction in range(3):
        stride = (1, 5, 17)[direction]
        owner_parts.append(jnp.broadcast_to(device[:, None], (devices, CAP)))
        slot_parts.append((within[None, :] - stride) % counts[:, None])
        owner_parts.append(jnp.broadcast_to(device[:, None], (devices, CAP)))
        slot_parts.append((within[None, :] + stride) % counts[:, None])
    owners = jnp.stack(owner_parts).reshape(-1).astype(jnp.int32)
    slot_ids = jnp.stack(slot_parts).reshape(-1).astype(jnp.int32)
    for direction in range(3):
        jump_list = [jump for jump in range(1, half + 1) if jump % 3 == direction]
        if len(jump_list) > 0:
            jumps = jnp.array(jump_list, dtype=jnp.int32)[None, :]
            grid_shape = (devices, len(jump_list))
            partner = row_of[:, None] * N_COL + (col_of[:, None] + jumps) % N_COL
            coin_flip = jax.random.randint(jax.random.fold_in(key_far, direction), grid_shape, 0, 4) < 3
            active = coin_flip | (col_of[:, None] == 0) | ((col_of[:, None] + jumps) % N_COL == 0)
            active = active & ((jumps < half) | (col_of[:, None] < half))
            place = 2 * ((jumps - 1) // 3)
            first_dev = jnp.broadcast_to(device[:, None], grid_shape).reshape(-1)
            first_pos = jnp.broadcast_to(place, grid_shape).reshape(-1)
            owners, slot_ids = rewire(owners, slot_ids, counts, first_dev, first_pos, partner.reshape(-1), first_pos + 1, direction, active.reshape(-1))
    flights = jax.random.randint(key_slab, (devices,), 1, KMAX + 1).astype(jnp.int32)
    flights = jnp.where(col_of == 0, KMAX, flights)
    upper_dev = (row_of + 1) % N_ROW * N_COL + col_of
    base_place = 2 * ((half + 2) // 3)
    turn = jnp.arange(KMAX, dtype=jnp.int32)[None, :]
    grid_shape = (devices, KMAX)
    active = turn < flights[:, None]
    first_dev = jnp.broadcast_to(device[:, None], grid_shape).reshape(-1)
    second_dev = jnp.broadcast_to(upper_dev[:, None], grid_shape).reshape(-1)
    first_pos = jnp.broadcast_to(base_place + 2 * turn, grid_shape).reshape(-1)
    owners, slot_ids = rewire(owners, slot_ids, counts, first_dev, first_pos, second_dev, first_pos + 1, 2, active.reshape(-1))
    numbers = (offsets[owners] + slot_ids).reshape(6, devices, CAP)
    is_live = within[None, :] < counts[:, None]
    named_blocks = jnp.where(is_live[None], numbers, -1).reshape(6, devices * CAP).astype(jnp.int32)
    return (counts, named_blocks)


def draw_block_counts(key, part):
    return forest_layout(key)[0]


def draw_neighbours(key, part):
    return forest_layout(key)[1]


def draw_conc(key, part):
    key = jax.random.fold_in(key, 7)
    coarse_estimate = jax.random.uniform(key, (SLOT_TOTAL_COUNT, 512), jnp.float32, -1.0, 1.0)
    return coarse_estimate


def place_ends(drawn, key, low, high):
    longest = drawn.shape.index(max(drawn.shape))
    spots = []
    for shift in (0, 1):
        where = [jax.random.randint(jax.random.fold_in(key, axis), (), 0, length) for axis, length in enumerate(drawn.shape)]
        where[longest] = (where[longest] + shift) % drawn.shape[longest]
        spots.append(tuple(where))
    return drawn.at[spots[0]].set(low).at[spots[1]].set(high)


def setup_inputs(seed: int = 0) -> dict:
    keys = jax.random.split(jax.random.key(seed), 6)
    conc = draw_conc(jax.random.fold_in(keys[5], 71), 0)
    levels = place_ends(jax.random.randint(keys[1], (SLOT_TOTAL_COUNT,), 0, 3), jax.random.fold_in(keys[1], 1), 0, 2).astype(jnp.int32)
    neighbours = draw_neighbours(jax.random.fold_in(keys[5], 71), 0)
    hanging = place_ends((jax.random.randint(keys[3], (6, SLOT_TOTAL_COUNT), 0, 4) < 1).astype(jnp.int32), jax.random.fold_in(keys[3], 1), 0, 1)
    block_counts = draw_block_counts(jax.random.fold_in(keys[5], 71), 0)
    return dict(conc=conc, levels=levels, neighbours=neighbours, hanging=hanging, block_counts=block_counts)


gradient_energy = 0.0625
time_step = 0.0004


def face_layers(cubes):
    blocks = cubes.shape[0]
    layers = [cubes[:, 0], cubes[:, 7], cubes[:, :, 0], cubes[:, :, 7], cubes[:, :, :, 0], cubes[:, :, :, 7]]
    return jnp.stack(layers, axis=1).reshape(blocks, 6, 64)


def coarsen(ghosts):
    grid_shape = ghosts.shape[:-1] + (4, 2, 4, 2)
    grouped = ghosts.reshape(grid_shape)
    summed = jnp.sum(grouped, axis=(-3, -1), keepdims=True) * 0.25
    return jnp.broadcast_to(summed, grid_shape).reshape(ghosts.shape)


def block_laplacian(cubes, ghosts, inverse_square):
    blocks = cubes.shape[0]
    sides = ghosts.reshape(blocks, 6, 8, 8)
    prev_x = jnp.concatenate([sides[:, 0][:, None], cubes[:, :7]], axis=1)
    next_x = jnp.concatenate([cubes[:, 1:], sides[:, 1][:, None]], axis=1)
    prev_y = jnp.concatenate([sides[:, 2][:, :, None], cubes[:, :, :7]], axis=2)
    following_ycoord = jnp.concatenate([cubes[:, :, 1:], sides[:, 3][:, :, None]], axis=2)
    prev_z = jnp.concatenate([sides[:, 4][:, :, :, None], cubes[:, :, :, :7]], axis=3)
    next_z = jnp.concatenate([cubes[:, :, :, 1:], sides[:, 5][:, :, :, None]], axis=3)
    summed = prev_x + next_x + prev_y + following_ycoord + prev_z + next_z - 6.0 * cubes
    return summed * inverse_square[:, None, None, None]


def reference(conc, levels, neighbours, hanging, block_counts):
    all_slots = conc.shape[0]
    devices = block_counts.shape[0]
    capacity = all_slots // devices
    offsets = (jnp.cumsum(block_counts) - block_counts).astype(jnp.int32)
    within = jnp.arange(capacity, dtype=jnp.int32)
    is_live = (within[None, :] < block_counts[:, None]).reshape(-1)
    numbers = (offsets[:, None] + within[None, :]).reshape(-1).astype(jnp.int32)
    live_total = AVG * DEVICES
    where_to = jnp.where(is_live, numbers, live_total).astype(jnp.int32)
    slot_of = jnp.zeros((live_total,), jnp.int32).at[where_to].set(jnp.arange(all_slots, dtype=jnp.int32), mode="drop")
    named_blocks = jnp.where(neighbours >= 0, neighbours, 0).astype(jnp.int32)
    source_slot = slot_of[named_blocks].T
    opposite = jnp.bitwise_xor(jnp.arange(6, dtype=jnp.int32), 1)[None, :]
    source_rows = (source_slot * 6 + opposite).astype(jnp.int32)
    coarse_flags = (hanging.T > 0)[:, :, None]
    inverse_square = jnp.left_shift(jnp.int32(1), 2 * levels).astype(jnp.float32)

    def laplacian(field):
        records = face_layers(field).reshape(all_slots * 6, 64)

        def one_device(pieces):
            cubes, rows_here, flags_here, inverse_here = pieces
            ghosts = records[rows_here.reshape(-1)].reshape(capacity, 6, 64)
            ghosts = jnp.where(flags_here, coarsen(ghosts), ghosts)
            return block_laplacian(cubes, ghosts, inverse_here)

        result = lax.map(one_device, (field.reshape(devices, capacity, 8, 8, 8), source_rows.reshape(devices, capacity, 6), coarse_flags.reshape(devices, capacity, 6, 1), inverse_square.reshape(devices, capacity)))
        return result.reshape(all_slots, 8, 8, 8)

    start = conc.reshape(all_slots, 8, 8, 8)
    first_mu = start * start * start - start - gradient_energy * laplacian(start)
    section_conc = start + time_step * laplacian(first_mu)
    second_mu = section_conc * section_conc * section_conc - section_conc - gradient_energy * laplacian(section_conc)
    finished = 0.5 * (start + section_conc + time_step * laplacian(second_mu))
    keep = is_live[:, None]
    conc_next = jnp.where(keep, finished.reshape(all_slots, 512), 0.0)
    potential = jnp.where(keep, second_mu.reshape(all_slots, 512), 0.0)
    return conc_next, potential
```

```python
import jax
import jax.numpy as jnp
from jax import lax
from jax.experimental import pallas as pl
from jax.experimental.pallas import tpu as pltpu
from jax.sharding import PartitionSpec as P

MESH = pl.DeviceIdType.MESH
gradient_energy = 0.0625
time_step = 0.0004

LANES = 128
FACES = 6 * LANES
X_RING = 4
SLAB = 32
ROUNDS = 4
BIG = 1e6
f32 = jnp.float32
bf16 = jnp.bfloat16


def iota(shape, dim):
    return lax.broadcasted_iota(jnp.int32, shape, dim)


def onehot(cond):
    return jnp.where(cond, 1.0, 0.0).astype(bf16)


def pieces(v):
    hi = v.astype(bf16)
    rest = v - hi.astype(f32)
    mid = rest.astype(bf16)
    lo = (rest - mid.astype(f32)).astype(bf16)
    return jnp.concatenate([hi, mid, lo], axis=0)


def turned(row):
    return jnp.broadcast_to(row, (LANES, LANES)).T


def layer_parts(ref):
    return [
        ref[0:64, :],
        ref[448:512, :],
        jnp.concatenate([ref[x * 64 : x * 64 + 8, :] for x in range(8)], axis=0),
        jnp.concatenate([ref[x * 64 + 56 : x * 64 + 64, :] for x in range(8)], axis=0),
        ref[pl.ds(0, 64, stride=8), :],
        ref[pl.ds(7, 64, stride=8), :],
    ]


def body(
    n_row, n_col,
    conc_ref, levels_ref, nb_ref, hang_ref, counts_ref,
    next_ref, pot_ref,
    pad_ref, ints_ref, off_ref, field_ref, conc_t_ref, section_ref, inner_ref, zbuf_ref, give_ref, take_ref, local_ref,
    send_ref, recv_ref, send_sem, recv_sem, slab_send_sem, slab_recv_sem,
):
    blocks = conc_ref.shape[0]
    z_ring = n_col // X_RING
    shift = z_ring // 4
    row = lax.axis_index("row")
    col = lax.axis_index("col")
    z = col // X_RING
    x = lax.rem(col, X_RING)
    below = lax.rem(row + n_row - 1, n_row)
    above = lax.rem(row + 1, n_row)

    def peer(dz, dx):
        return lax.rem(z + dz, z_ring) * X_RING + lax.rem(x + dx, X_RING)

    def line(dz, dx):
        return lax.rem(dz + shift, z_ring) * X_RING + dx

    own_line = shift * X_RING
    for r in range(ROUNDS):
        recv_ref[r, own_line : own_line + 1, :] = jnp.zeros((1, LANES), f32)
        recv_ref[r, n_col + SLAB :, :] = jnp.zeros((2 * LANES - n_col - SLAB, LANES), f32)

    barrier = pltpu.get_barrier_semaphore()

    def greet(j, carry):
        pl.semaphore_signal(
            barrier, inc=1, device_id={"col": peer(j // X_RING, lax.rem(j, X_RING))}, device_id_type=MESH
        )
        return carry

    lax.fori_loop(1, n_col, greet, 0)
    for other in (below, above):
        pl.semaphore_signal(barrier, inc=1, device_id={"row": other}, device_id_type=MESH)

    counts = counts_ref[...].astype(f32)
    before = onehot(iota((n_col, n_col), 0) < iota((n_col, n_col), 1))
    partial = jnp.dot(counts.astype(bf16), before, preferred_element_type=f32)
    totals = jnp.sum(counts, axis=1, keepdims=True)
    start = jnp.zeros((1, 1), f32)
    for r in range(n_row):
        off_ref[r : r + 1, :] = partial[r : r + 1, :] + start
        start = start + totals[r : r + 1, :]
    lane = iota((1, LANES), 1)
    mine = lane == col

    def pick(v):
        return jnp.sum(jnp.where(mine, v, 0.0), axis=1, keepdims=True)

    def ranges(r):
        offsets = off_ref[pl.ds(r, 1), :]
        held = counts_ref[pl.ds(r, 1), :].astype(f32)
        return offsets, held

    off_row, held_row = ranges(row)
    off_low, held_low = (pick(v) for v in ranges(below))
    off_high, held_high = (pick(v) for v in ranges(above))
    my_count = pick(held_row)
    row_start = off_row[:, 0:1]
    row_end = row_start + jnp.sum(held_row, axis=1, keepdims=True)
    off_turned = turned(off_row)

    pad_ref[0:blocks, :] = conc_ref[...]
    pad_ref[blocks:, :] = jnp.zeros((LANES - blocks, 512), f32)
    live_rows = iota((LANES, 512), 0).astype(f32) < my_count
    start_field = jnp.where(live_rows, pad_ref[...], 0.0).T
    field_ref[...] = start_field
    conc_t_ref[...] = start_field

    ints_ref[0:8, :] = jnp.full((8, LANES), -1, jnp.int32)
    ints_ref[8:24, :] = jnp.zeros((16, LANES), jnp.int32)
    ints_ref[0:6, 0:blocks] = nb_ref[...]
    ints_ref[8:14, 0:blocks] = hang_ref[...]
    ints_ref[16:17, 0:blocks] = levels_ref[...]
    level = ints_ref[16:17, :]
    scale = jnp.where(level == 0, 1.0, jnp.where(level == 1, 4.0, jnp.where(level == 2, 16.0, 0.0)))
    hanging = jnp.concatenate([ints_ref[8 + f : 9 + f, :] for f in range(6)], axis=1) > 0

    partner_parts, give_parts, take_parts, slab_give, slab_take, low_parts, high_parts = [], [], [], [], [], [], []
    for f in range(6):
        target = ints_ref[f : f + 1, :].astype(f32)
        live = (target >= 0.0) & (lane.astype(f32) < my_count)
        in_row = live & (target >= row_start) & (target < row_end)
        reached = off_turned <= target
        owner = jnp.sum(jnp.where(reached, 1.0, 0.0), axis=0, keepdims=True).astype(jnp.int32) - 1
        first = jnp.max(jnp.where(reached, off_turned, 0.0), axis=0, keepdims=True)
        here = in_row & (owner == col)
        far = in_row & (owner != col)
        low = live & (target >= off_low) & (target < off_low + held_low)
        high = live & (target >= off_high) & (target < off_high + held_high)
        slot = jnp.where(in_row, target - first, jnp.where(low, target - off_low, target - off_high))
        apart = (((owner >> 2) - z + shift) & (z_ring - 1)) * X_RING + ((owner - x) & (X_RING - 1))
        partner_parts.append(jnp.where(far, apart, -1))
        give_key = (lane + f * LANES).astype(f32)
        take_key = slot + float((f ^ 1) * LANES)
        give_parts.append(give_key)
        take_parts.append(take_key)
        slab_give.append(jnp.where(low, give_key, jnp.where(high, give_key + 1024.0, BIG)))
        slab_take.append(jnp.where(low, take_key, jnp.where(high, take_key + 1024.0, BIG)))
        low_parts.append(jnp.where(low, 1.0, 0.0))
        high_parts.append(jnp.where(high, 1.0, 0.0))
        local_ref[f * LANES : (f + 1) * LANES, :] = onehot(
            (iota((LANES, LANES), 0).astype(f32) == slot) & here
        )
    partner = jnp.concatenate(partner_parts, axis=1)
    low_all = jnp.concatenate(low_parts, axis=1)
    high_all = jnp.concatenate(high_parts, axis=1)
    matched = iota((n_col, FACES), 0) == partner
    slab_line = iota((SLAB, FACES), 0)
    slab_id = (slab_line + jnp.where(slab_line >= SLAB // 2, SLAB // 2, 0)).astype(f32)
    n_low = jnp.sum(low_all, axis=1, keepdims=True)
    for ref, stride, keys, slab_keys in (
        (give_ref, n_col + SLAB, give_parts, slab_give),
        (take_ref, 2 * LANES, take_parts, slab_take),
    ):
        key = jnp.concatenate(keys, axis=1)
        least = jnp.min(jnp.where(matched, key, BIG), axis=1, keepdims=True)
        ref[0:n_col, :] = onehot(matched & (key == least))
        ref[stride : stride + n_col, :] = onehot(matched & (key != least))
        slab_key = jnp.concatenate(slab_keys, axis=1)
        smaller = jnp.zeros((1, FACES), f32)
        for f in range(6):
            smaller = smaller + jnp.sum(
                jnp.where(turned(slab_keys[f])[:, 0:1] < slab_key, 1.0, 0.0), axis=0, keepdims=True
            )
        place = jnp.where(low_all > 0.0, smaller, jnp.where(high_all > 0.0, smaller - n_low + SLAB, -1.0))
        ref[n_col : n_col + SLAB, :] = onehot(slab_id == place)
        ref[stride + n_col : stride + n_col + SLAB, :] = onehot(slab_id + SLAB // 2 == place)
    take_ref[n_col + SLAB : 2 * LANES, :] = jnp.zeros((2 * LANES - n_col - SLAB, FACES), bf16)
    take_ref[2 * LANES + n_col + SLAB :, :] = jnp.zeros((2 * LANES - n_col - SLAB, FACES), bf16)
    zbuf_ref[...] = jnp.zeros((512, LANES), f32)

    pl.semaphore_wait(barrier, n_col + 1)

    def start_copy(r, dz, dx):
        pltpu.make_async_remote_copy(
            src_ref=send_ref.at[r, pl.ds(line(dz, dx), 1)],
            dst_ref=recv_ref.at[r, pl.ds(line(z_ring - dz, lax.rem(X_RING - dx, X_RING)), 1)],
            send_sem=send_sem.at[r],
            recv_sem=recv_sem.at[r],
            device_id={"col": peer(dz, dx)},
            device_id_type=MESH,
        ).start()

    def slab_copy(r, side, other):
        half = SLAB // 2
        return pltpu.make_async_remote_copy(
            src_ref=send_ref.at[r, pl.ds(n_col + side * half, half)],
            dst_ref=recv_ref.at[r, pl.ds(n_col + (1 - side) * half, half)],
            send_sem=slab_send_sem.at[r, side],
            recv_sem=slab_recv_sem.at[r, side],
            device_id={"row": other},
            device_id_type=MESH,
        )

    def all_lines(r):
        return pltpu.make_async_remote_copy(
            src_ref=send_ref.at[r, pl.ds(0, n_col - 1)],
            dst_ref=recv_ref.at[r, pl.ds(0, n_col - 1)],
            send_sem=send_sem.at[r],
            recv_sem=recv_sem.at[r],
            device_id={"col": peer(1, 0)},
            device_id_type=MESH,
        )

    def laplacian(r):
        layers = layer_parts(field_ref)
        cut = pieces(jnp.concatenate(layers, axis=1))
        given = lax.dot_general(give_ref[...], cut, (((1,), (1,)), ((), ())), preferred_element_type=f32)
        given = given[:, 0:64] + (given[:, 64:128] + given[:, 128:192])
        lines = n_col + SLAB
        send_ref[r, :, 0:64] = given[0:lines]
        send_ref[r, :, 64:128] = given[lines : 2 * lines]
        for dx in range(X_RING):
            start_copy(r, z_ring // 2, dx)

        def outward(i, carry):
            near = z_ring // 2 - i
            for dx in range(X_RING):
                start_copy(r, near, dx)
                start_copy(r, z_ring - near, dx)
            return carry

        lax.fori_loop(1, z_ring // 2, outward, 0)
        for dx in range(1, X_RING):
            start_copy(r, 0, dx)
        slabs = [slab_copy(r, 0, below), slab_copy(r, 1, above)]
        for copy in slabs:
            copy.start()

        cells = field_ref[...]
        cube = cells.reshape(8, 8, 8, LANES)
        zero_x = jnp.zeros((1, 8, 8, LANES), f32)
        zero_y = jnp.zeros((8, 1, 8, LANES), f32)
        summed = jnp.concatenate([zero_x, cube[:7]], axis=0) + jnp.concatenate([cube[1:], zero_x], axis=0)
        summed = summed + jnp.concatenate([zero_y, cube[:, :7]], axis=1)
        summed = summed + jnp.concatenate([cube[:, 1:], zero_y], axis=1)
        columns = cells.reshape(64, 8, LANES)
        z_at = iota((64, 8, LANES), 1)
        prev_z = jnp.where(z_at > 0, pltpu.roll(columns, 1, 1), 0.0)
        next_z = jnp.where(z_at < 7, pltpu.roll(columns, 7, 1), 0.0)
        inner_ref[...] = summed.reshape(512, LANES) + (prev_z + next_z).reshape(512, LANES) - 6.0 * cells
        near_ghosts = []
        for f in range(6):
            g = f ^ 1
            part = jnp.dot(
                cut[:, g * LANES : (g + 1) * LANES],
                local_ref[f * LANES : (f + 1) * LANES, :],
                preferred_element_type=f32,
            )
            near_ghosts.append(part[0:64] + (part[64:128] + part[128:192]))
        ghosts = jnp.concatenate(near_ghosts, axis=1)

        all_lines(r).wait_recv()
        for copy in slabs:
            copy.wait_recv()
        taken = recv_ref[r].T
        taken = pieces(jnp.concatenate([taken[0:64], taken[64:128]], axis=1))
        taken = jnp.dot(taken, take_ref[...], preferred_element_type=f32)
        ghosts = ghosts + (taken[0:64] + (taken[64:128] + taken[128:192]))
        pairs = ghosts.reshape(4, 2, 8, FACES)
        pairs = pairs[:, 0] + pairs[:, 1]
        even = iota((4, 8, FACES), 1) % 2 == 0
        pairs = 0.25 * (pairs + jnp.where(even, pltpu.roll(pairs, 7, 1), pltpu.roll(pairs, 1, 1)))
        coarse = jnp.broadcast_to(pairs[:, None], (4, 2, 8, FACES)).reshape(64, FACES)
        ghosts = jnp.where(hanging, coarse, ghosts)

        sides = [ghosts[:, f * LANES : (f + 1) * LANES] for f in range(6)]
        inner_ref[0:64, :] += sides[0]
        inner_ref[448:512, :] += sides[1]
        for i in range(8):
            inner_ref[i * 64 : i * 64 + 8, :] += sides[2][i * 8 : i * 8 + 8]
            inner_ref[i * 64 + 56 : i * 64 + 64, :] += sides[3][i * 8 : i * 8 + 8]
        zbuf_ref[pl.ds(0, 64, stride=8), :] = sides[4]
        zbuf_ref[pl.ds(7, 64, stride=8), :] = sides[5]
        return (inner_ref[...] + zbuf_ref[...]) * scale

    def potential(v, lap):
        return v * v * v - v - gradient_energy * lap

    field_ref[...] = potential(conc_t_ref[...], laplacian(0))
    section = conc_t_ref[...] + time_step * laplacian(1)
    section_ref[...] = section
    field_ref[...] = section
    second = potential(section_ref[...], laplacian(2))
    field_ref[...] = second
    finished = 0.5 * (conc_t_ref[...] + section_ref[...] + time_step * laplacian(3))
    pot_ref[...] = field_ref[...].T[0:blocks]
    next_ref[...] = finished.T[0:blocks]
    for r in range(ROUNDS):
        all_lines(r).wait_send()
        slab_copy(r, 0, below).wait_send()
        slab_copy(r, 1, above).wait_send()


def per_device(n_row, n_col):
    def run(conc, levels, neighbours, hanging, block_counts):
        blocks = conc.shape[0]
        vmem = pl.BlockSpec(memory_space=pltpu.VMEM)
        lines = n_col + SLAB
        whole = pltpu.VMEM((512, LANES), f32)

        def kernel(*refs):
            body(n_row, n_col, *refs)

        return pl.pallas_call(
            kernel,
            out_shape=[jax.ShapeDtypeStruct((blocks, 512), f32)] * 2,
            in_specs=[vmem] * 5,
            out_specs=[vmem] * 2,
            scratch_shapes=[
                pltpu.VMEM((LANES, 512), f32),
                pltpu.VMEM((24, LANES), jnp.int32),
                pltpu.VMEM((n_row, n_col), f32),
                whole, whole, whole, whole, whole,
                pltpu.VMEM((2 * lines, FACES), bf16),
                pltpu.VMEM((4 * LANES, FACES), bf16),
                pltpu.VMEM((FACES, LANES), bf16),
                pltpu.VMEM((ROUNDS, lines, LANES), f32),
                pltpu.VMEM((ROUNDS, 2 * LANES, LANES), f32),
                pltpu.SemaphoreType.DMA((ROUNDS,)),
                pltpu.SemaphoreType.DMA((ROUNDS,)),
                pltpu.SemaphoreType.DMA((ROUNDS, 2)),
                pltpu.SemaphoreType.DMA((ROUNDS, 2)),
            ],
            compiler_params=pltpu.CompilerParams(
                collective_id=0, has_side_effects=True, vmem_limit_bytes=32 * 1024 * 1024
            ),
        )(conc, levels.reshape(1, blocks), neighbours, hanging, block_counts.reshape(n_row, n_col))

    return run


def solution(mesh):
    return jax.shard_map(
        per_device(mesh.shape["row"], mesh.shape["col"]),
        mesh=mesh,
        in_specs=(
            P(("row", "col"), None),
            P(("row", "col")),
            P(None, ("row", "col")),
            P(None, ("row", "col")),
            P(),
        ),
        out_specs=(P(("row", "col"), None), P(("row", "col"), None)),
        check_vma=False,
    )
```

```python
import jax
import jax.numpy as jnp
from jax import lax
from jax.experimental import pallas as pl
from jax.experimental.pallas import tpu as pltpu
from jax.sharding import PartitionSpec as P

MESH = pl.DeviceIdType.MESH
gradient_energy = 0.0625
time_step = 0.0004

LANES = 128
FACES = 6 * LANES
X_RING = 4
SLAB = 32
ROUNDS = 4
OUTER_FIRST = (2, 1, 3, 0)
BIG = 1e6
f32 = jnp.float32
bf16 = jnp.bfloat16


def iota(shape, dim):
    return lax.broadcasted_iota(jnp.int32, shape, dim)


def onehot(cond):
    return jnp.where(cond, 1.0, 0.0).astype(bf16)


def pieces(v):
    hi = v.astype(bf16)
    rest = v - hi.astype(f32)
    mid = rest.astype(bf16)
    lo = (rest - mid.astype(f32)).astype(bf16)
    return jnp.concatenate([hi, mid, lo], axis=0)


def turned(row):
    return jnp.broadcast_to(row, (LANES, LANES)).T


def layer_parts(ref):
    return [
        ref[0:64, :],
        ref[448:512, :],
        jnp.concatenate([ref[x * 64 : x * 64 + 8, :] for x in range(8)], axis=0),
        jnp.concatenate([ref[x * 64 + 56 : x * 64 + 64, :] for x in range(8)], axis=0),
        ref[pl.ds(0, 64, stride=8), :],
        ref[pl.ds(7, 64, stride=8), :],
    ]


def body(
    n_row, n_col,
    conc_ref, levels_ref, nb_ref, hang_ref, counts_ref,
    next_ref, pot_ref,
    conc_in, pad_ref, levels_in, nb_in, hang_in, counts_in, load_sem,
    ints_ref, off_ref, field_ref, conc_t_ref, section_ref, inner_ref, zbuf_ref, give_ref, take_ref, local_ref,
    send_ref, recv_ref, send_sem, recv_sem, slab_send_sem, slab_recv_sem,
):
    blocks = conc_ref.shape[0]
    z_ring = n_col // X_RING
    shift = z_ring // 4
    half = n_col // 2
    row = lax.axis_index("row")
    col = lax.axis_index("col")
    z = col // X_RING
    x = lax.rem(col, X_RING)
    below = lax.rem(row + n_row - 1, n_row)
    above = lax.rem(row + 1, n_row)

    def peer(dz, dx):
        return lax.rem(z + dz, z_ring) * X_RING + lax.rem(x + dx, X_RING)

    def line(dz, dx):
        return lax.rem(dz + shift, z_ring) * X_RING + dx

    own_line = shift * X_RING
    for r in range(ROUNDS):
        recv_ref[r, own_line : own_line + 1, :] = jnp.zeros((1, LANES), f32)

    barrier = pltpu.get_barrier_semaphore()

    def greet(dz, dx):
        pl.semaphore_signal(barrier, inc=1, device_id={"col": peer(dz, dx)}, device_id_type=MESH)

    def greet_pair(i, carry):
        away = z_ring // 2 - i
        for dx in OUTER_FIRST:
            greet(away, dx)
            greet(z_ring - away, dx)
        return carry

    for dx in OUTER_FIRST:
        greet(z_ring // 2, dx)
    lax.fori_loop(1, z_ring // 2, greet_pair, 0)
    for dx in range(1, X_RING):
        greet(0, dx)
    for other in (below, above):
        pl.semaphore_signal(barrier, inc=1, device_id={"row": other}, device_id_type=MESH)

    loads = [
        pltpu.make_async_copy(src, dst, load_sem.at[i])
        for i, (src, dst) in enumerate(
            (
                (counts_ref, counts_in),
                (nb_ref, nb_in),
                (conc_ref, conc_in),
                (hang_ref, hang_in),
                (levels_ref, levels_in),
            )
        )
    ]
    for load in loads:
        load.start()
    for load in loads:
        load.wait()

    counts = counts_in[...].astype(f32)
    before = onehot(iota((n_col, n_col), 0) < iota((n_col, n_col), 1))
    partial = jnp.dot(counts.astype(bf16), before, preferred_element_type=f32)
    totals = jnp.sum(counts, axis=1, keepdims=True)
    start = jnp.zeros((1, 1), f32)
    for r in range(n_row):
        off_ref[r : r + 1, :] = partial[r : r + 1, :] + start
        start = start + totals[r : r + 1, :]
    lane = iota((1, LANES), 1)
    mine = lane == col

    def pick(v):
        return jnp.sum(jnp.where(mine, v, 0.0), axis=1, keepdims=True)

    def ranges(r):
        offsets = off_ref[pl.ds(r, 1), :]
        held = counts_in[pl.ds(r, 1), :].astype(f32)
        return offsets, held

    off_row, held_row = ranges(row)
    off_low, held_low = (pick(v) for v in ranges(below))
    off_high, held_high = (pick(v) for v in ranges(above))
    my_count = pick(held_row)
    row_start = off_row[:, 0:1]
    row_end = row_start + jnp.sum(held_row, axis=1, keepdims=True)
    off_turned = turned(off_row)

    pad_ref[0:blocks, :] = conc_in[...]
    pad_ref[blocks:, :] = jnp.zeros((LANES - blocks, 512), f32)
    live_rows = iota((LANES, 512), 0).astype(f32) < my_count
    start_field = jnp.where(live_rows, pad_ref[...], 0.0).T
    field_ref[...] = start_field
    conc_t_ref[...] = start_field

    ints_ref[0:8, :] = jnp.full((8, LANES), -1, jnp.int32)
    ints_ref[8:24, :] = jnp.zeros((16, LANES), jnp.int32)
    ints_ref[0:6, 0:blocks] = nb_in[...]
    ints_ref[8:14, 0:blocks] = hang_in[...]
    ints_ref[16:17, 0:blocks] = levels_in[...]
    level = ints_ref[16:17, :]
    scale = jnp.where(level == 0, 1.0, jnp.where(level == 1, 4.0, jnp.where(level == 2, 16.0, 0.0)))
    hanging = jnp.concatenate([ints_ref[8 + f : 9 + f, :] for f in range(6)], axis=1) > 0

    partner_parts, give_parts, take_parts, slab_give, slab_take, low_parts, high_parts = [], [], [], [], [], [], []
    for f in range(6):
        target = ints_ref[f : f + 1, :].astype(f32)
        live = (target >= 0.0) & (lane.astype(f32) < my_count)
        in_row = live & (target >= row_start) & (target < row_end)
        reached = off_turned <= target
        owner = jnp.sum(jnp.where(reached, 1.0, 0.0), axis=0, keepdims=True).astype(jnp.int32) - 1
        first = jnp.max(jnp.where(reached, off_turned, 0.0), axis=0, keepdims=True)
        here = in_row & (owner == col)
        far = in_row & (owner != col)
        low = live & (target >= off_low) & (target < off_low + held_low)
        high = live & (target >= off_high) & (target < off_high + held_high)
        slot = jnp.where(in_row, target - first, jnp.where(low, target - off_low, target - off_high))
        apart = (((owner >> 2) - z + shift) & (z_ring - 1)) * X_RING + ((owner - x) & (X_RING - 1))
        partner_parts.append(jnp.where(far, apart, -1))
        give_key = (lane + f * LANES).astype(f32)
        take_key = slot + float((f ^ 1) * LANES)
        give_parts.append(give_key)
        take_parts.append(take_key)
        slab_give.append(jnp.where(low, give_key, jnp.where(high, give_key + 1024.0, BIG)))
        slab_take.append(jnp.where(low, take_key, jnp.where(high, take_key + 1024.0, BIG)))
        low_parts.append(jnp.where(low, 1.0, 0.0))
        high_parts.append(jnp.where(high, 1.0, 0.0))
        local_ref[f * LANES : (f + 1) * LANES, :] = onehot(
            (iota((LANES, LANES), 0).astype(f32) == slot) & here
        )
    partner = jnp.concatenate(partner_parts, axis=1)
    low_all = jnp.concatenate(low_parts, axis=1)
    high_all = jnp.concatenate(high_parts, axis=1)
    matched = iota((n_col, FACES), 0) == partner
    slab_line = iota((SLAB, FACES), 0)
    slab_id = (slab_line + jnp.where(slab_line >= SLAB // 2, SLAB // 2, 0)).astype(f32)
    n_low = jnp.sum(low_all, axis=1, keepdims=True)
    for ref, keys, slab_keys in ((give_ref, give_parts, slab_give), (take_ref, take_parts, slab_take)):
        key = jnp.concatenate(keys, axis=1)
        least = jnp.min(jnp.where(matched, key, BIG), axis=1, keepdims=True)
        for i, lines in enumerate((onehot(matched & (key == least)), onehot(matched & (key != least)))):
            ref[i * half : (i + 1) * half, :] = lines[half:]
            ref[n_col + i * half : n_col + (i + 1) * half, :] = lines[:half]
        slab_key = jnp.concatenate(slab_keys, axis=1)
        smaller = jnp.zeros((1, FACES), f32)
        for f in range(6):
            smaller = smaller + jnp.sum(
                jnp.where(turned(slab_keys[f])[:, 0:1] < slab_key, 1.0, 0.0), axis=0, keepdims=True
            )
        place = jnp.where(low_all > 0.0, smaller, jnp.where(high_all > 0.0, smaller - n_low + SLAB, -1.0))
        ref[2 * n_col : 2 * n_col + SLAB, :] = onehot(slab_id == place)
        ref[2 * n_col + SLAB : 2 * n_col + 2 * SLAB, :] = onehot(slab_id + SLAB // 2 == place)
    zbuf_ref[...] = jnp.zeros((512, LANES), f32)

    pl.semaphore_wait(barrier, n_col + 1)

    def start_copy(r, dz, dx, far):
        pltpu.make_async_remote_copy(
            src_ref=send_ref.at[r, pl.ds(line(dz, dx), 1)],
            dst_ref=recv_ref.at[r, pl.ds(line(z_ring - dz, lax.rem(X_RING - dx, X_RING)), 1)],
            send_sem=send_sem.at[r],
            recv_sem=recv_sem.at[r, far],
            device_id={"col": peer(dz, dx)},
            device_id_type=MESH,
        ).start()

    def slab_copy(r, side, other):
        part = SLAB // 2
        return pltpu.make_async_remote_copy(
            src_ref=send_ref.at[r, pl.ds(n_col + side * part, part)],
            dst_ref=recv_ref.at[r, pl.ds(n_col + (1 - side) * part, part)],
            send_sem=slab_send_sem.at[r, side],
            recv_sem=slab_recv_sem.at[r, side],
            device_id={"row": other},
            device_id_type=MESH,
        )

    def lines_in(r, far, count):
        return pltpu.make_async_remote_copy(
            src_ref=send_ref.at[r, pl.ds(0, count)],
            dst_ref=recv_ref.at[r, pl.ds(0, count)],
            send_sem=send_sem.at[r],
            recv_sem=recv_sem.at[r, far],
            device_id={"col": peer(1, 0)},
            device_id_type=MESH,
        )

    def summed(v):
        return v[0:64] + (v[64:128] + v[128:192])

    def by_cell(lines):
        turned_lines = lines.T
        return jnp.concatenate([turned_lines[0:64], turned_lines[64:128]], axis=1)

    def laplacian(r):
        layers = layer_parts(field_ref)
        cut = pieces(jnp.concatenate(layers, axis=1))

        def give(first, last):
            given = lax.dot_general(
                give_ref[first:last, :], cut, (((1,), (1,)), ((), ())), preferred_element_type=f32
            )
            return given[:, 0:64] + (given[:, 64:128] + given[:, 128:192])

        def outward(far):
            def step(away, carry):
                for dx in OUTER_FIRST:
                    start_copy(r, away, dx, far)
                    start_copy(r, z_ring - away, dx, far)
                return carry

            return lambda i, carry: step(z_ring // 2 - i, carry)

        given = give(0, n_col)
        send_ref[r, half:n_col, 0:64] = given[0:half]
        send_ref[r, half:n_col, 64:128] = given[half:n_col]
        for dx in OUTER_FIRST:
            start_copy(r, z_ring // 2, dx, 1)
        lax.fori_loop(1, z_ring // 2 - shift, outward(1), 0)
        for dx in OUTER_FIRST:
            start_copy(r, shift, dx, 0)
        given = give(n_col, 2 * n_col + 2 * SLAB)
        send_ref[r, 0:half, 0:64] = given[0:half]
        send_ref[r, 0:half, 64:128] = given[half:n_col]
        send_ref[r, n_col:, 0:64] = given[n_col : n_col + SLAB]
        send_ref[r, n_col:, 64:128] = given[n_col + SLAB :]
        for dx in OUTER_FIRST:
            start_copy(r, z_ring - shift, dx, 1)
        lax.fori_loop(z_ring // 2 - shift + 1, z_ring // 2, outward(0), 0)
        for dx in range(1, X_RING):
            start_copy(r, 0, dx, 0)
        slabs = [slab_copy(r, 0, below), slab_copy(r, 1, above)]
        for copy in slabs:
            copy.start()

        cells = field_ref[...]
        cube = cells.reshape(8, 8, 8, LANES)
        zero_x = jnp.zeros((1, 8, 8, LANES), f32)
        zero_y = jnp.zeros((8, 1, 8, LANES), f32)
        steps = jnp.concatenate([zero_x, cube[:7]], axis=0) + jnp.concatenate([cube[1:], zero_x], axis=0)
        steps = steps + jnp.concatenate([zero_y, cube[:, :7]], axis=1)
        steps = steps + jnp.concatenate([cube[:, 1:], zero_y], axis=1)
        columns = cells.reshape(64, 8, LANES)
        z_at = iota((64, 8, LANES), 1)
        prev_z = jnp.where(z_at > 0, pltpu.roll(columns, 1, 1), 0.0)
        next_z = jnp.where(z_at < 7, pltpu.roll(columns, 7, 1), 0.0)
        inner_ref[...] = steps.reshape(512, LANES) + (prev_z + next_z).reshape(512, LANES) - 6.0 * cells
        near_ghosts = []
        for f in range(6):
            g = f ^ 1
            part = jnp.dot(
                cut[:, g * LANES : (g + 1) * LANES],
                local_ref[f * LANES : (f + 1) * LANES, :],
                preferred_element_type=f32,
            )
            near_ghosts.append(summed(part))
        ghosts = jnp.concatenate(near_ghosts, axis=1)

        if r == ROUNDS - 1:
            pot_ref[...] = cells.T[0:blocks]

        lines_in(r, 0, half - 1).wait_recv()
        for copy in slabs:
            copy.wait_recv()
        taken = jnp.concatenate([by_cell(recv_ref[r, 0:half, :]), by_cell(recv_ref[r, n_col:, :])], axis=1)
        ghosts = ghosts + summed(
            jnp.dot(pieces(taken), take_ref[n_col:, :], preferred_element_type=f32)
        )
        lines_in(r, 1, half).wait_recv()
        taken = by_cell(recv_ref[r, half:n_col, :])
        ghosts = ghosts + summed(
            jnp.dot(pieces(taken), take_ref[0:n_col, :], preferred_element_type=f32)
        )
        pairs = ghosts.reshape(4, 2, 8, FACES)
        pairs = pairs[:, 0] + pairs[:, 1]
        even = iota((4, 8, FACES), 1) % 2 == 0
        pairs = 0.25 * (pairs + jnp.where(even, pltpu.roll(pairs, 7, 1), pltpu.roll(pairs, 1, 1)))
        coarse = jnp.broadcast_to(pairs[:, None], (4, 2, 8, FACES)).reshape(64, FACES)
        ghosts = jnp.where(hanging, coarse, ghosts)

        sides = [ghosts[:, f * LANES : (f + 1) * LANES] for f in range(6)]
        inner_ref[0:64, :] += sides[0]
        inner_ref[448:512, :] += sides[1]
        for i in range(8):
            inner_ref[i * 64 : i * 64 + 8, :] += sides[2][i * 8 : i * 8 + 8]
            inner_ref[i * 64 + 56 : i * 64 + 64, :] += sides[3][i * 8 : i * 8 + 8]
        zbuf_ref[pl.ds(0, 64, stride=8), :] = sides[4]
        zbuf_ref[pl.ds(7, 64, stride=8), :] = sides[5]
        return (inner_ref[...] + zbuf_ref[...]) * scale

    def potential(v, lap):
        return v * v * v - v - gradient_energy * lap

    field_ref[...] = potential(conc_t_ref[...], laplacian(0))
    section = conc_t_ref[...] + time_step * laplacian(1)
    section_ref[...] = section
    field_ref[...] = section
    second = potential(section_ref[...], laplacian(2))
    field_ref[...] = second
    finished = 0.5 * (conc_t_ref[...] + section_ref[...] + time_step * laplacian(3))
    next_ref[...] = finished.T[0:blocks]
    for r in range(ROUNDS):
        lines_in(r, 0, n_col - 1).wait_send()
        slab_copy(r, 0, below).wait_send()
        slab_copy(r, 1, above).wait_send()


def per_device(n_row, n_col):
    def run(conc, levels, neighbours, hanging, block_counts):
        blocks = conc.shape[0]
        vmem = pl.BlockSpec(memory_space=pltpu.VMEM)
        lines = n_col + SLAB
        whole = pltpu.VMEM((512, LANES), f32)

        def kernel(*refs):
            body(n_row, n_col, *refs)

        return pl.pallas_call(
            kernel,
            out_shape=[pltpu.VMEM((blocks, 512), f32)] * 2,
            in_specs=[pl.BlockSpec(memory_space=pltpu.HBM)] * 5,
            out_specs=[vmem] * 2,
            scratch_shapes=[
                pltpu.VMEM((blocks, 512), f32),
                pltpu.VMEM((LANES, 512), f32),
                pltpu.VMEM((1, blocks), jnp.int32),
                pltpu.VMEM((6, blocks), jnp.int32),
                pltpu.VMEM((6, blocks), jnp.int32),
                pltpu.VMEM((n_row, n_col), jnp.int32),
                pltpu.SemaphoreType.DMA((5,)),
                pltpu.VMEM((24, LANES), jnp.int32),
                pltpu.VMEM((n_row, n_col), f32),
                whole, whole, whole, whole, whole,
                pltpu.VMEM((2 * lines, FACES), bf16),
                pltpu.VMEM((2 * lines, FACES), bf16),
                pltpu.VMEM((FACES, LANES), bf16),
                pltpu.VMEM((ROUNDS, lines, LANES), f32),
                pltpu.VMEM((ROUNDS, lines, LANES), f32),
                pltpu.SemaphoreType.DMA((ROUNDS,)),
                pltpu.SemaphoreType.DMA((ROUNDS, 2)),
                pltpu.SemaphoreType.DMA((ROUNDS, 2)),
                pltpu.SemaphoreType.DMA((ROUNDS, 2)),
            ],
            compiler_params=pltpu.CompilerParams(
                collective_id=0, has_side_effects=True, vmem_limit_bytes=32 * 1024 * 1024
            ),
        )(
            *(
                pltpu.with_memory_space_constraint(v, pltpu.HBM)
                for v in (conc, levels.reshape(1, blocks), neighbours, hanging, block_counts.reshape(n_row, n_col))
            )
        )

    return run


def solution(mesh):
    return jax.shard_map(
        per_device(mesh.shape["row"], mesh.shape["col"]),
        mesh=mesh,
        in_specs=(
            P(("row", "col"), None),
            P(("row", "col")),
            P(None, ("row", "col")),
            P(None, ("row", "col")),
            P(),
        ),
        out_specs=(P(("row", "col"), None), P(("row", "col"), None)),
        check_vma=False,
    )
```

```python
import jax
import jax.numpy as jnp
from jax import lax
from jax.experimental import pallas as pl
from jax.experimental.pallas import tpu as pltpu
from jax.sharding import PartitionSpec as P

MESH = pl.DeviceIdType.MESH
gradient_energy = 0.0625
time_step = 0.0004

LANES = 128
FACES = 6 * LANES
X_RING = 4
SLAB = 32
ROUNDS = 4
OUTER_FIRST = (2, 1, 3, 0)
BIG = 1e6
f32 = jnp.float32
bf16 = jnp.bfloat16


def iota(shape, dim):
    return lax.broadcasted_iota(jnp.int32, shape, dim)


def onehot(cond):
    return jnp.where(cond, 1.0, 0.0).astype(bf16)


def pieces(v):
    hi = v.astype(bf16)
    rest = v - hi.astype(f32)
    mid = rest.astype(bf16)
    lo = (rest - mid.astype(f32)).astype(bf16)
    return jnp.concatenate([hi, mid, lo], axis=0)


def turned(row):
    return jnp.broadcast_to(row, (LANES, LANES)).T


def layer_parts(ref):
    return [
        ref[0:64, :],
        ref[448:512, :],
        jnp.concatenate([ref[x * 64 : x * 64 + 8, :] for x in range(8)], axis=0),
        jnp.concatenate([ref[x * 64 + 56 : x * 64 + 64, :] for x in range(8)], axis=0),
        ref[pl.ds(0, 64, stride=8), :],
        ref[pl.ds(7, 64, stride=8), :],
    ]


def body(
    n_row, n_col,
    conc_ref, levels_ref, nb_ref, hang_ref, counts_ref,
    next_ref, pot_ref,
    conc_in, pad_ref, levels_in, nb_in, hang_in, counts_in, load_sem,
    ints_ref, off_ref, field_ref, conc_t_ref, section_ref, inner_ref, zbuf_ref, give_ref, take_ref, local_ref,
    send_ref, recv_ref, mid_ref, send_sem, recv_sem, slab_send_sem, slab_recv_sem, mid_send_sem, mid_recv_sem,
):
    blocks = conc_ref.shape[0]
    z_ring = n_col // X_RING
    shift = z_ring // 4
    half = n_col // 2
    row = lax.axis_index("row")
    col = lax.axis_index("col")
    z = col // X_RING
    x = lax.rem(col, X_RING)
    below = lax.rem(row + n_row - 1, n_row)
    above = lax.rem(row + 1, n_row)

    def peer(dz, dx):
        return lax.rem(z + dz, z_ring) * X_RING + lax.rem(x + dx, X_RING)

    def line(dz, dx):
        return lax.rem(dz + shift, z_ring) * X_RING + dx

    own_line = shift * X_RING
    for r in range(ROUNDS):
        recv_ref[r, own_line : own_line + 1, :] = jnp.zeros((1, LANES), f32)

    barrier = pltpu.get_barrier_semaphore()

    def greet(dz, dx):
        pl.semaphore_signal(barrier, inc=1, device_id={"col": peer(dz, dx)}, device_id_type=MESH)

    def greet_pair(i, carry):
        away = shift + 1 - i
        for dx in OUTER_FIRST:
            greet(away, dx)
            greet(z_ring - away, dx)
        return carry

    lax.fori_loop(1, shift + 1, greet_pair, 0)
    for dx in range(1, X_RING):
        greet(0, dx)
    for other in (below, above):
        pl.semaphore_signal(barrier, inc=1, device_id={"row": other}, device_id_type=MESH)

    loads = [
        pltpu.make_async_copy(src, dst, load_sem.at[i])
        for i, (src, dst) in enumerate(
            (
                (counts_ref, counts_in),
                (nb_ref, nb_in),
                (conc_ref, conc_in),
                (hang_ref, hang_in),
                (levels_ref, levels_in),
            )
        )
    ]
    for load in loads:
        load.start()
    for load in loads:
        load.wait()

    counts = counts_in[...].astype(f32)
    before = onehot(iota((n_col, n_col), 0) < iota((n_col, n_col), 1))
    partial = jnp.dot(counts.astype(bf16), before, preferred_element_type=f32)
    totals = jnp.sum(counts, axis=1, keepdims=True)
    start = jnp.zeros((1, 1), f32)
    for r in range(n_row):
        off_ref[r : r + 1, :] = partial[r : r + 1, :] + start
        start = start + totals[r : r + 1, :]
    lane = iota((1, LANES), 1)
    mine = lane == col

    def pick(v):
        return jnp.sum(jnp.where(mine, v, 0.0), axis=1, keepdims=True)

    def ranges(r):
        offsets = off_ref[pl.ds(r, 1), :]
        held = counts_in[pl.ds(r, 1), :].astype(f32)
        return offsets, held

    off_row, held_row = ranges(row)
    off_low, held_low = (pick(v) for v in ranges(below))
    off_high, held_high = (pick(v) for v in ranges(above))
    my_count = pick(held_row)
    row_start = off_row[:, 0:1]
    row_end = row_start + jnp.sum(held_row, axis=1, keepdims=True)
    off_turned = turned(off_row)

    pad_ref[0:blocks, :] = conc_in[...]
    pad_ref[blocks:, :] = jnp.zeros((LANES - blocks, 512), f32)
    live_rows = iota((LANES, 512), 0).astype(f32) < my_count
    start_field = jnp.where(live_rows, pad_ref[...], 0.0).T
    field_ref[...] = start_field
    conc_t_ref[...] = start_field

    ints_ref[0:8, :] = jnp.full((8, LANES), -1, jnp.int32)
    ints_ref[8:24, :] = jnp.zeros((16, LANES), jnp.int32)
    ints_ref[0:6, 0:blocks] = nb_in[...]
    ints_ref[8:14, 0:blocks] = hang_in[...]
    ints_ref[16:17, 0:blocks] = levels_in[...]
    level = ints_ref[16:17, :]
    scale = jnp.where(level == 0, 1.0, jnp.where(level == 1, 4.0, jnp.where(level == 2, 16.0, 0.0)))
    hanging = jnp.concatenate([ints_ref[8 + f : 9 + f, :] for f in range(6)], axis=1) > 0

    partner_parts, give_parts, take_parts, slab_give, slab_take, low_parts, high_parts = [], [], [], [], [], [], []
    for f in range(6):
        target = ints_ref[f : f + 1, :].astype(f32)
        live = (target >= 0.0) & (lane.astype(f32) < my_count)
        in_row = live & (target >= row_start) & (target < row_end)
        reached = off_turned <= target
        owner = jnp.sum(jnp.where(reached, 1.0, 0.0), axis=0, keepdims=True).astype(jnp.int32) - 1
        first = jnp.max(jnp.where(reached, off_turned, 0.0), axis=0, keepdims=True)
        here = in_row & (owner == col)
        far = in_row & (owner != col)
        low = live & (target >= off_low) & (target < off_low + held_low)
        high = live & (target >= off_high) & (target < off_high + held_high)
        slot = jnp.where(in_row, target - first, jnp.where(low, target - off_low, target - off_high))
        apart = (((owner >> 2) - z + shift) & (z_ring - 1)) * X_RING + ((owner - x) & (X_RING - 1))
        partner_parts.append(jnp.where(far, apart, -1))
        give_key = (lane + f * LANES).astype(f32)
        take_key = slot + float((f ^ 1) * LANES)
        give_parts.append(give_key)
        take_parts.append(take_key)
        slab_give.append(jnp.where(low, give_key, jnp.where(high, give_key + 1024.0, BIG)))
        slab_take.append(jnp.where(low, take_key, jnp.where(high, take_key + 1024.0, BIG)))
        low_parts.append(jnp.where(low, 1.0, 0.0))
        high_parts.append(jnp.where(high, 1.0, 0.0))
        local_ref[f * LANES : (f + 1) * LANES, :] = onehot(
            (iota((LANES, LANES), 0).astype(f32) == slot) & here
        )
    partner = jnp.concatenate(partner_parts, axis=1)
    low_all = jnp.concatenate(low_parts, axis=1)
    high_all = jnp.concatenate(high_parts, axis=1)
    matched = iota((n_col, FACES), 0) == partner
    slab_line = iota((SLAB, FACES), 0)
    slab_id = (slab_line + jnp.where(slab_line >= SLAB // 2, SLAB // 2, 0)).astype(f32)
    n_low = jnp.sum(low_all, axis=1, keepdims=True)
    for ref, keys, slab_keys in ((give_ref, give_parts, slab_give), (take_ref, take_parts, slab_take)):
        key = jnp.concatenate(keys, axis=1)
        least = jnp.min(jnp.where(matched, key, BIG), axis=1, keepdims=True)
        for i, lines in enumerate((onehot(matched & (key == least)), onehot(matched & (key != least)))):
            ref[i * half : (i + 1) * half, :] = lines[half:]
            ref[n_col + i * half : n_col + (i + 1) * half, :] = lines[:half]
        slab_key = jnp.concatenate(slab_keys, axis=1)
        smaller = jnp.zeros((1, FACES), f32)
        for f in range(6):
            smaller = smaller + jnp.sum(
                jnp.where(turned(slab_keys[f])[:, 0:1] < slab_key, 1.0, 0.0), axis=0, keepdims=True
            )
        place = jnp.where(low_all > 0.0, smaller, jnp.where(high_all > 0.0, smaller - n_low + SLAB, -1.0))
        ref[2 * n_col : 2 * n_col + SLAB, :] = onehot(slab_id == place)
        ref[2 * n_col + SLAB : 2 * n_col + 2 * SLAB, :] = onehot(slab_id + SLAB // 2 == place)
    zbuf_ref[...] = jnp.zeros((512, LANES), f32)

    pl.semaphore_wait(barrier, (2 * shift + 1) * X_RING + 1)

    def start_copy(r, dz, dx, far, left=None):
        pltpu.make_async_remote_copy(
            src_ref=(send_ref.at[r] if left is None else mid_ref).at[pl.ds(line(dz, dx), 1)],
            dst_ref=recv_ref.at[r, pl.ds(line(z_ring - dz, lax.rem(X_RING - dx, X_RING)), 1)],
            send_sem=send_sem.at[r],
            recv_sem=recv_sem.at[r, far],
            device_id={"col": peer(dz if left is None else left, dx)},
            device_id_type=MESH,
        ).start()

    def bundle(dz):
        lines = pl.ds(line(2 * dz, 0), 2 * X_RING)
        return pltpu.make_async_remote_copy(
            src_ref=send_ref.at[0, lines],
            dst_ref=mid_ref.at[lines],
            send_sem=mid_send_sem,
            recv_sem=mid_recv_sem,
            device_id={"col": peer(dz, 0)},
            device_id_type=MESH,
        )

    def bundles_in():
        lines = pl.ds(0, (z_ring // 2 - 1) * 2 * X_RING)
        return pltpu.make_async_remote_copy(
            src_ref=send_ref.at[0, lines],
            dst_ref=mid_ref.at[lines],
            send_sem=mid_send_sem,
            recv_sem=mid_recv_sem,
            device_id={"col": peer(1, 0)},
            device_id_type=MESH,
        )

    def relay():
        bundle(z_ring - shift).start()

        def first_leg(i, carry):
            bundle(shift - i).start()
            bundle(z_ring - shift + i).start()
            return carry

        lax.fori_loop(1, shift, first_leg, 0)
        for dz in (1, z_ring - 1, 0):
            for dx in OUTER_FIRST:
                if dz or dx:
                    start_copy(0, dz, dx, 0)
        slabs = [slab_copy(0, 0, below), slab_copy(0, 1, above)]
        for copy in slabs:
            copy.start()
        bundles_in().wait_recv()
        for dx in OUTER_FIRST:
            start_copy(0, z_ring // 2, dx, 1, z_ring - shift)

        def second_leg(far):
            def step(i, carry):
                away = z_ring // 2 - i
                for dx in OUTER_FIRST:
                    start_copy(0, away, dx, far, (away + 1) // 2)
                    start_copy(0, z_ring - away, dx, far, lax.rem(z_ring - away // 2, z_ring))
                return carry

            return step

        lax.fori_loop(1, z_ring // 2 - shift, second_leg(1), 0)
        for dx in OUTER_FIRST:
            start_copy(0, shift, dx, 0, shift // 2)
            start_copy(0, z_ring - shift, dx, 1, z_ring - shift // 2)
        lax.fori_loop(z_ring // 2 - shift + 1, z_ring // 2 - 1, second_leg(0), 0)
        return slabs

    def slab_copy(r, side, other):
        part = SLAB // 2
        return pltpu.make_async_remote_copy(
            src_ref=send_ref.at[r, pl.ds(n_col + side * part, part)],
            dst_ref=recv_ref.at[r, pl.ds(n_col + (1 - side) * part, part)],
            send_sem=slab_send_sem.at[r, side],
            recv_sem=slab_recv_sem.at[r, side],
            device_id={"row": other},
            device_id_type=MESH,
        )

    def lines_in(r, far, count):
        return pltpu.make_async_remote_copy(
            src_ref=send_ref.at[r, pl.ds(0, count)],
            dst_ref=recv_ref.at[r, pl.ds(0, count)],
            send_sem=send_sem.at[r],
            recv_sem=recv_sem.at[r, far],
            device_id={"col": peer(1, 0)},
            device_id_type=MESH,
        )

    def summed(v):
        return v[0:64] + (v[64:128] + v[128:192])

    def by_cell(lines):
        turned_lines = lines.T
        return jnp.concatenate([turned_lines[0:64], turned_lines[64:128]], axis=1)

    def laplacian(r):
        layers = layer_parts(field_ref)
        cut = pieces(jnp.concatenate(layers, axis=1))

        def give(first, last):
            given = lax.dot_general(
                give_ref[first:last, :], cut, (((1,), (1,)), ((), ())), preferred_element_type=f32
            )
            return given[:, 0:64] + (given[:, 64:128] + given[:, 128:192])

        def outward(far):
            def step(away, carry):
                for dx in OUTER_FIRST:
                    start_copy(r, away, dx, far)
                    start_copy(r, z_ring - away, dx, far)
                return carry

            return lambda i, carry: step(z_ring // 2 - i, carry)

        given = give(0, n_col)
        send_ref[r, half:n_col, 0:64] = given[0:half]
        send_ref[r, half:n_col, 64:128] = given[half:n_col]
        if r > 0:
            for dx in OUTER_FIRST:
                start_copy(r, z_ring // 2, dx, 1)
            lax.fori_loop(1, z_ring // 2 - shift, outward(1), 0)
            for dx in OUTER_FIRST:
                start_copy(r, shift, dx, 0)
        given = give(n_col, 2 * n_col + 2 * SLAB)
        send_ref[r, 0:half, 0:64] = given[0:half]
        send_ref[r, 0:half, 64:128] = given[half:n_col]
        send_ref[r, n_col:, 0:64] = given[n_col : n_col + SLAB]
        send_ref[r, n_col:, 64:128] = given[n_col + SLAB :]
        if r > 0:
            for dx in OUTER_FIRST:
                start_copy(r, z_ring - shift, dx, 1)
            lax.fori_loop(z_ring // 2 - shift + 1, z_ring // 2, outward(0), 0)
            for dx in range(1, X_RING):
                start_copy(r, 0, dx, 0)
            slabs = [slab_copy(r, 0, below), slab_copy(r, 1, above)]
            for copy in slabs:
                copy.start()
        else:
            slabs = relay()

        cells = field_ref[...]
        cube = cells.reshape(8, 8, 8, LANES)
        zero_x = jnp.zeros((1, 8, 8, LANES), f32)
        zero_y = jnp.zeros((8, 1, 8, LANES), f32)
        steps = jnp.concatenate([zero_x, cube[:7]], axis=0) + jnp.concatenate([cube[1:], zero_x], axis=0)
        steps = steps + jnp.concatenate([zero_y, cube[:, :7]], axis=1)
        steps = steps + jnp.concatenate([cube[:, 1:], zero_y], axis=1)
        columns = cells.reshape(64, 8, LANES)
        z_at = iota((64, 8, LANES), 1)
        prev_z = jnp.where(z_at > 0, pltpu.roll(columns, 1, 1), 0.0)
        next_z = jnp.where(z_at < 7, pltpu.roll(columns, 7, 1), 0.0)
        inner_ref[...] = steps.reshape(512, LANES) + (prev_z + next_z).reshape(512, LANES) - 6.0 * cells
        near_ghosts = []
        for f in range(6):
            g = f ^ 1
            part = jnp.dot(
                cut[:, g * LANES : (g + 1) * LANES],
                local_ref[f * LANES : (f + 1) * LANES, :],
                preferred_element_type=f32,
            )
            near_ghosts.append(summed(part))
        ghosts = jnp.concatenate(near_ghosts, axis=1)

        if r == ROUNDS - 1:
            pot_ref[...] = cells.T[0:blocks]

        lines_in(r, 0, half - 1).wait_recv()
        for copy in slabs:
            copy.wait_recv()
        taken = jnp.concatenate([by_cell(recv_ref[r, 0:half, :]), by_cell(recv_ref[r, n_col:, :])], axis=1)
        ghosts = ghosts + summed(
            jnp.dot(pieces(taken), take_ref[n_col:, :], preferred_element_type=f32)
        )
        lines_in(r, 1, half).wait_recv()
        taken = by_cell(recv_ref[r, half:n_col, :])
        ghosts = ghosts + summed(
            jnp.dot(pieces(taken), take_ref[0:n_col, :], preferred_element_type=f32)
        )
        pairs = ghosts.reshape(4, 2, 8, FACES)
        pairs = pairs[:, 0] + pairs[:, 1]
        even = iota((4, 8, FACES), 1) % 2 == 0
        pairs = 0.25 * (pairs + jnp.where(even, pltpu.roll(pairs, 7, 1), pltpu.roll(pairs, 1, 1)))
        coarse = jnp.broadcast_to(pairs[:, None], (4, 2, 8, FACES)).reshape(64, FACES)
        ghosts = jnp.where(hanging, coarse, ghosts)

        sides = [ghosts[:, f * LANES : (f + 1) * LANES] for f in range(6)]
        inner_ref[0:64, :] += sides[0]
        inner_ref[448:512, :] += sides[1]
        for i in range(8):
            inner_ref[i * 64 : i * 64 + 8, :] += sides[2][i * 8 : i * 8 + 8]
            inner_ref[i * 64 + 56 : i * 64 + 64, :] += sides[3][i * 8 : i * 8 + 8]
        zbuf_ref[pl.ds(0, 64, stride=8), :] = sides[4]
        zbuf_ref[pl.ds(7, 64, stride=8), :] = sides[5]
        return (inner_ref[...] + zbuf_ref[...]) * scale

    def potential(v, lap):
        return v * v * v - v - gradient_energy * lap

    field_ref[...] = potential(conc_t_ref[...], laplacian(0))
    section = conc_t_ref[...] + time_step * laplacian(1)
    section_ref[...] = section
    field_ref[...] = section
    second = potential(section_ref[...], laplacian(2))
    field_ref[...] = second
    finished = 0.5 * (conc_t_ref[...] + section_ref[...] + time_step * laplacian(3))
    next_ref[...] = finished.T[0:blocks]
    bundles_in().wait_send()
    for r in range(ROUNDS):
        lines_in(r, 0, n_col - 1).wait_send()
        slab_copy(r, 0, below).wait_send()
        slab_copy(r, 1, above).wait_send()


def per_device(n_row, n_col):
    def run(conc, levels, neighbours, hanging, block_counts):
        blocks = conc.shape[0]
        vmem = pl.BlockSpec(memory_space=pltpu.VMEM)
        lines = n_col + SLAB
        whole = pltpu.VMEM((512, LANES), f32)

        def kernel(*refs):
            body(n_row, n_col, *refs)

        return pl.pallas_call(
            kernel,
            out_shape=[pltpu.VMEM((blocks, 512), f32)] * 2,
            in_specs=[pl.BlockSpec(memory_space=pltpu.HBM)] * 5,
            out_specs=[vmem] * 2,
            scratch_shapes=[
                pltpu.VMEM((blocks, 512), f32),
                pltpu.VMEM((LANES, 512), f32),
                pltpu.VMEM((1, blocks), jnp.int32),
                pltpu.VMEM((6, blocks), jnp.int32),
                pltpu.VMEM((6, blocks), jnp.int32),
                pltpu.VMEM((n_row, n_col), jnp.int32),
                pltpu.SemaphoreType.DMA((5,)),
                pltpu.VMEM((24, LANES), jnp.int32),
                pltpu.VMEM((n_row, n_col), f32),
                whole, whole, whole, whole, whole,
                pltpu.VMEM((2 * lines, FACES), bf16),
                pltpu.VMEM((2 * lines, FACES), bf16),
                pltpu.VMEM((FACES, LANES), bf16),
                pltpu.VMEM((ROUNDS, lines, LANES), f32),
                pltpu.VMEM((ROUNDS, lines, LANES), f32),
                pltpu.VMEM((n_col, LANES), f32),
                pltpu.SemaphoreType.DMA((ROUNDS,)),
                pltpu.SemaphoreType.DMA((ROUNDS, 2)),
                pltpu.SemaphoreType.DMA((ROUNDS, 2)),
                pltpu.SemaphoreType.DMA((ROUNDS, 2)),
                pltpu.SemaphoreType.DMA,
                pltpu.SemaphoreType.DMA,
            ],
            compiler_params=pltpu.CompilerParams(
                collective_id=0, has_side_effects=True, vmem_limit_bytes=32 * 1024 * 1024
            ),
        )(
            *(
                pltpu.with_memory_space_constraint(v, pltpu.HBM)
                for v in (conc, levels.reshape(1, blocks), neighbours, hanging, block_counts.reshape(n_row, n_col))
            )
        )

    return run


def solution(mesh):
    return jax.shard_map(
        per_device(mesh.shape["row"], mesh.shape["col"]),
        mesh=mesh,
        in_specs=(
            P(("row", "col"), None),
            P(("row", "col")),
            P(None, ("row", "col")),
            P(None, ("row", "col")),
            P(),
        ),
        out_specs=(P(("row", "col"), None), P(("row", "col"), None)),
        check_vma=False,
    )
```

```python
import jax
import jax.numpy as jnp
from jax import lax
from jax.experimental import pallas as pl
from jax.experimental.pallas import tpu as pltpu
from jax.sharding import PartitionSpec as P

MESH = pl.DeviceIdType.MESH
gradient_energy = 0.0625
time_step = 0.0004

LANES = 128
FACES = 6 * LANES
X_RING = 4
SLAB = 32
ROUNDS = 4
OUTER_FIRST = (2, 1, 3, 0)
BIG = 1e6
f32 = jnp.float32
bf16 = jnp.bfloat16


def iota(shape, dim):
    return lax.broadcasted_iota(jnp.int32, shape, dim)


def onehot(cond):
    return jnp.where(cond, 1.0, 0.0).astype(bf16)


def pieces(v):
    hi = v.astype(bf16)
    rest = v - hi.astype(f32)
    mid = rest.astype(bf16)
    lo = (rest - mid.astype(f32)).astype(bf16)
    return jnp.concatenate([hi, mid, lo], axis=0)


def turned(row):
    return jnp.broadcast_to(row, (LANES, LANES)).T


def layer_parts(ref):
    return [
        ref[0:64, :],
        ref[448:512, :],
        jnp.concatenate([ref[x * 64 : x * 64 + 8, :] for x in range(8)], axis=0),
        jnp.concatenate([ref[x * 64 + 56 : x * 64 + 64, :] for x in range(8)], axis=0),
        ref[pl.ds(0, 64, stride=8), :],
        ref[pl.ds(7, 64, stride=8), :],
    ]


def body(
    n_row, n_col,
    conc_ref, levels_ref, nb_ref, hang_ref, counts_ref,
    out_ref,
    conc_in, pad_ref, levels_in, nb_in, hang_in, counts_in, load_sem,
    ints_ref, off_ref, field_ref, conc_t_ref, section_ref, inner_ref, zbuf_ref, give_ref, take_ref, local_ref,
    send_ref, recv_ref, mid_ref, send_sem, recv_sem, slab_send_sem, slab_recv_sem, mid_send_sem, mid_recv_sem, hello_sem,
):
    blocks = conc_ref.shape[0]
    z_ring = n_col // X_RING
    shift = z_ring // 4
    half = n_col // 2
    row = lax.axis_index("row")
    col = lax.axis_index("col")
    z = col // X_RING
    x = lax.rem(col, X_RING)
    below = lax.rem(row + n_row - 1, n_row)
    above = lax.rem(row + 1, n_row)

    def peer(dz, dx):
        return lax.rem(z + dz, z_ring) * X_RING + lax.rem(x + dx, X_RING)

    def line(dz, dx):
        return lax.rem(dz + shift, z_ring) * X_RING + dx

    own_line = shift * X_RING
    for r in range(ROUNDS):
        recv_ref[r, own_line : own_line + 1, :] = jnp.zeros((1, LANES), f32)

    barrier = pltpu.get_barrier_semaphore()

    def greet(dz, dx):
        pl.semaphore_signal(barrier, inc=1, device_id={"col": peer(dz, dx)}, device_id_type=MESH)

    def greet_pair(i, carry):
        greet(shift + 1 - i, 0)
        greet(z_ring - shift - 1 + i, 0)
        return carry

    lax.fori_loop(1, shift + 1, greet_pair, 0)
    for dx in range(1, X_RING):
        greet(0, dx)
    for other in (below, above):
        pl.semaphore_signal(barrier, inc=1, device_id={"row": other}, device_id_type=MESH)

    loads = [
        pltpu.make_async_copy(src, dst, load_sem.at[i])
        for i, (src, dst) in enumerate(
            (
                (counts_ref, counts_in),
                (nb_ref, nb_in),
                (conc_ref, conc_in),
                (hang_ref, hang_in),
                (levels_ref, levels_in),
            )
        )
    ]
    for load in loads:
        load.start()
    for load in loads:
        load.wait()

    counts = counts_in[...].astype(f32)
    before = onehot(iota((n_col, n_col), 0) < iota((n_col, n_col), 1))
    partial = jnp.dot(counts.astype(bf16), before, preferred_element_type=f32)
    totals = jnp.sum(counts, axis=1, keepdims=True)
    start = jnp.zeros((1, 1), f32)
    for r in range(n_row):
        off_ref[r : r + 1, :] = partial[r : r + 1, :] + start
        start = start + totals[r : r + 1, :]
    lane = iota((1, LANES), 1)
    mine = lane == col

    def pick(v):
        return jnp.sum(jnp.where(mine, v, 0.0), axis=1, keepdims=True)

    def ranges(r):
        offsets = off_ref[pl.ds(r, 1), :]
        held = counts_in[pl.ds(r, 1), :].astype(f32)
        return offsets, held

    off_row, held_row = ranges(row)
    off_low, held_low = (pick(v) for v in ranges(below))
    off_high, held_high = (pick(v) for v in ranges(above))
    my_count = pick(held_row)
    row_start = off_row[:, 0:1]
    row_end = row_start + jnp.sum(held_row, axis=1, keepdims=True)
    off_turned = turned(off_row)

    pad_ref[0:blocks, :] = conc_in[...]
    pad_ref[blocks:, :] = jnp.zeros((LANES - blocks, 512), f32)
    live_rows = iota((LANES, 512), 0).astype(f32) < my_count
    start_field = jnp.where(live_rows, pad_ref[...], 0.0).T
    field_ref[...] = start_field
    conc_t_ref[...] = start_field

    ints_ref[0:8, :] = jnp.full((8, LANES), -1, jnp.int32)
    ints_ref[8:24, :] = jnp.zeros((16, LANES), jnp.int32)
    ints_ref[0:6, 0:blocks] = nb_in[...]
    ints_ref[8:14, 0:blocks] = hang_in[...]
    ints_ref[16:17, 0:blocks] = levels_in[...]
    level = ints_ref[16:17, :]
    scale = jnp.where(level == 0, 1.0, jnp.where(level == 1, 4.0, jnp.where(level == 2, 16.0, 0.0)))
    hanging = jnp.concatenate([ints_ref[8 + f : 9 + f, :] for f in range(6)], axis=1) > 0

    partner_parts, give_parts, take_parts, slab_give, slab_take, low_parts, high_parts = [], [], [], [], [], [], []
    for f in range(6):
        target = ints_ref[f : f + 1, :].astype(f32)
        live = (target >= 0.0) & (lane.astype(f32) < my_count)
        in_row = live & (target >= row_start) & (target < row_end)
        reached = off_turned <= target
        owner = jnp.sum(jnp.where(reached, 1.0, 0.0), axis=0, keepdims=True).astype(jnp.int32) - 1
        first = jnp.max(jnp.where(reached, off_turned, 0.0), axis=0, keepdims=True)
        here = in_row & (owner == col)
        far = in_row & (owner != col)
        low = live & (target >= off_low) & (target < off_low + held_low)
        high = live & (target >= off_high) & (target < off_high + held_high)
        slot = jnp.where(in_row, target - first, jnp.where(low, target - off_low, target - off_high))
        apart = (((owner >> 2) - z + shift) & (z_ring - 1)) * X_RING + ((owner - x) & (X_RING - 1))
        partner_parts.append(jnp.where(far, apart, -1))
        give_key = (lane + f * LANES).astype(f32)
        take_key = slot + float((f ^ 1) * LANES)
        give_parts.append(give_key)
        take_parts.append(take_key)
        slab_give.append(jnp.where(low, give_key, jnp.where(high, give_key + 1024.0, BIG)))
        slab_take.append(jnp.where(low, take_key, jnp.where(high, take_key + 1024.0, BIG)))
        low_parts.append(jnp.where(low, 1.0, 0.0))
        high_parts.append(jnp.where(high, 1.0, 0.0))
        local_ref[f * LANES : (f + 1) * LANES, :] = onehot(
            (iota((LANES, LANES), 0).astype(f32) == slot) & here
        )
    partner = jnp.concatenate(partner_parts, axis=1)
    low_all = jnp.concatenate(low_parts, axis=1)
    high_all = jnp.concatenate(high_parts, axis=1)
    matched = iota((n_col, FACES), 0) == partner
    slab_line = iota((SLAB, FACES), 0)
    slab_id = (slab_line + jnp.where(slab_line >= SLAB // 2, SLAB // 2, 0)).astype(f32)
    n_low = jnp.sum(low_all, axis=1, keepdims=True)
    for ref, keys, slab_keys in ((give_ref, give_parts, slab_give), (take_ref, take_parts, slab_take)):
        key = jnp.concatenate(keys, axis=1)
        least = jnp.min(jnp.where(matched, key, BIG), axis=1, keepdims=True)
        for i, lines in enumerate((onehot(matched & (key == least)), onehot(matched & (key != least)))):
            ref[i * half : (i + 1) * half, :] = lines[half:]
            ref[n_col + i * half : n_col + (i + 1) * half, :] = lines[:half]
        slab_key = jnp.concatenate(slab_keys, axis=1)
        smaller = jnp.zeros((1, FACES), f32)
        for f in range(6):
            smaller = smaller + jnp.sum(
                jnp.where(turned(slab_keys[f])[:, 0:1] < slab_key, 1.0, 0.0), axis=0, keepdims=True
            )
        place = jnp.where(low_all > 0.0, smaller, jnp.where(high_all > 0.0, smaller - n_low + SLAB, -1.0))
        ref[2 * n_col : 2 * n_col + SLAB, :] = onehot(slab_id == place)
        ref[2 * n_col + SLAB : 2 * n_col + 2 * SLAB, :] = onehot(slab_id + SLAB // 2 == place)
    zbuf_ref[...] = jnp.zeros((512, LANES), f32)


    def start_copy(r, dz, dx, far, left=None):
        pltpu.make_async_remote_copy(
            src_ref=(send_ref.at[r] if left is None else mid_ref).at[pl.ds(line(dz, dx), 1)],
            dst_ref=recv_ref.at[r, pl.ds(line(z_ring - dz, lax.rem(X_RING - dx, X_RING)), 1)],
            send_sem=send_sem.at[r],
            recv_sem=recv_sem.at[r, far],
            device_id={"col": peer(dz if left is None else left, dx)},
            device_id_type=MESH,
        ).start()

    def bundle(dz):
        lines = pl.ds(line(2 * dz, 0), 2 * X_RING)
        return pltpu.make_async_remote_copy(
            src_ref=send_ref.at[0, lines],
            dst_ref=mid_ref.at[lines],
            send_sem=mid_send_sem,
            recv_sem=mid_recv_sem,
            device_id={"col": peer(dz, 0)},
            device_id_type=MESH,
        )

    def bundles_in():
        lines = pl.ds(0, (z_ring // 2 - 1) * 2 * X_RING)
        return pltpu.make_async_remote_copy(
            src_ref=send_ref.at[0, lines],
            dst_ref=mid_ref.at[lines],
            send_sem=mid_send_sem,
            recv_sem=mid_recv_sem,
            device_id={"col": peer(1, 0)},
            device_id_type=MESH,
        )

    def relay():
        pl.semaphore_wait(barrier, 2 * shift + X_RING - 1 + 2)
        bundle(z_ring - shift).start()
        pl.semaphore_signal(hello_sem, inc=1, device_id={"col": peer(shift, 0)}, device_id_type=MESH)

        def first_leg(i, carry):
            bundle(shift - i).start()
            bundle(z_ring - shift + i).start()
            return carry

        lax.fori_loop(1, shift, first_leg, 0)
        slabs = [slab_copy(0, 0, below), slab_copy(0, 1, above)]
        for copy in slabs:
            copy.start()
        pl.semaphore_wait(hello_sem, 1)
        bundles_in().wait_recv()
        for dx in OUTER_FIRST:
            start_copy(0, z_ring // 2, dx, 1, z_ring - shift)

        def second_leg(far):
            def step(i, carry):
                away = z_ring // 2 - i
                for dx in OUTER_FIRST:
                    start_copy(0, away, dx, far, (away + 1) // 2)
                    start_copy(0, z_ring - away, dx, far, lax.rem(z_ring - away // 2, z_ring))
                return carry

            return step

        lax.fori_loop(1, z_ring // 2 - shift, second_leg(1), 0)
        for dx in OUTER_FIRST:
            start_copy(0, shift, dx, 0, shift // 2)
            start_copy(0, z_ring - shift, dx, 1, z_ring - shift // 2)
        lax.fori_loop(z_ring // 2 - shift + 1, z_ring // 2 - 1, second_leg(0), 0)
        for dz in (1, z_ring - 1, 0):
            for dx in OUTER_FIRST:
                if dz or dx:
                    start_copy(0, dz, dx, 0)
        return slabs

    def slab_copy(r, side, other):
        part = SLAB // 2
        return pltpu.make_async_remote_copy(
            src_ref=send_ref.at[r, pl.ds(n_col + side * part, part)],
            dst_ref=recv_ref.at[r, pl.ds(n_col + (1 - side) * part, part)],
            send_sem=slab_send_sem.at[r, side],
            recv_sem=slab_recv_sem.at[r, side],
            device_id={"row": other},
            device_id_type=MESH,
        )

    def lines_in(r, far, count):
        return pltpu.make_async_remote_copy(
            src_ref=send_ref.at[r, pl.ds(0, count)],
            dst_ref=recv_ref.at[r, pl.ds(0, count)],
            send_sem=send_sem.at[r],
            recv_sem=recv_sem.at[r, far],
            device_id={"col": peer(1, 0)},
            device_id_type=MESH,
        )

    def summed(v):
        return v[0:64] + (v[64:128] + v[128:192])

    def by_cell(lines):
        turned_lines = lines.T
        return jnp.concatenate([turned_lines[0:64], turned_lines[64:128]], axis=1)

    def laplacian(r):
        layers = layer_parts(field_ref)
        cut = pieces(jnp.concatenate(layers, axis=1))

        def give(first, last):
            given = lax.dot_general(
                give_ref[first:last, :], cut, (((1,), (1,)), ((), ())), preferred_element_type=f32
            )
            return given[:, 0:64] + (given[:, 64:128] + given[:, 128:192])

        def outward(far):
            def step(away, carry):
                for dx in OUTER_FIRST:
                    start_copy(r, away, dx, far)
                    start_copy(r, z_ring - away, dx, far)
                return carry

            return lambda i, carry: step(z_ring // 2 - i, carry)

        given = give(0, n_col)
        send_ref[r, half:n_col, 0:64] = given[0:half]
        send_ref[r, half:n_col, 64:128] = given[half:n_col]
        if r > 0:
            for dx in OUTER_FIRST:
                start_copy(r, z_ring // 2, dx, 1)
            lax.fori_loop(1, z_ring // 2 - shift, outward(1), 0)
            for dx in OUTER_FIRST:
                start_copy(r, shift, dx, 0)
        given = give(n_col, 2 * n_col + 2 * SLAB)
        send_ref[r, 0:half, 0:64] = given[0:half]
        send_ref[r, 0:half, 64:128] = given[half:n_col]
        send_ref[r, n_col:, 0:64] = given[n_col : n_col + SLAB]
        send_ref[r, n_col:, 64:128] = given[n_col + SLAB :]
        if r > 0:
            for dx in OUTER_FIRST:
                start_copy(r, z_ring - shift, dx, 1)
            lax.fori_loop(z_ring // 2 - shift + 1, z_ring // 2, outward(0), 0)
            for dx in range(1, X_RING):
                start_copy(r, 0, dx, 0)
            slabs = [slab_copy(r, 0, below), slab_copy(r, 1, above)]
            for copy in slabs:
                copy.start()
        else:
            slabs = relay()

        cells = field_ref[...]
        cube = cells.reshape(8, 8, 8, LANES)
        zero_x = jnp.zeros((1, 8, 8, LANES), f32)
        zero_y = jnp.zeros((8, 1, 8, LANES), f32)
        steps = jnp.concatenate([zero_x, cube[:7]], axis=0) + jnp.concatenate([cube[1:], zero_x], axis=0)
        steps = steps + jnp.concatenate([zero_y, cube[:, :7]], axis=1)
        steps = steps + jnp.concatenate([cube[:, 1:], zero_y], axis=1)
        columns = cells.reshape(64, 8, LANES)
        z_at = iota((64, 8, LANES), 1)
        prev_z = jnp.where(z_at > 0, pltpu.roll(columns, 1, 1), 0.0)
        next_z = jnp.where(z_at < 7, pltpu.roll(columns, 7, 1), 0.0)
        inner_ref[...] = steps.reshape(512, LANES) + (prev_z + next_z).reshape(512, LANES) - 6.0 * cells
        near_ghosts = []
        for f in range(6):
            g = f ^ 1
            part = jnp.dot(
                cut[:, g * LANES : (g + 1) * LANES],
                local_ref[f * LANES : (f + 1) * LANES, :],
                preferred_element_type=f32,
            )
            near_ghosts.append(summed(part))
        ghosts = jnp.concatenate(near_ghosts, axis=1)

        if r == ROUNDS - 1:
            out_ref[1] = cells.T
            bundles_in().wait_send()
            for done in range(ROUNDS):
                lines_in(done, 0, n_col - 1).wait_send()
                slab_copy(done, 0, below).wait_send()
                slab_copy(done, 1, above).wait_send()

        lines_in(r, 0, half - 1).wait_recv()
        for copy in slabs:
            copy.wait_recv()
        taken = jnp.concatenate([by_cell(recv_ref[r, 0:half, :]), by_cell(recv_ref[r, n_col:, :])], axis=1)
        ghosts = ghosts + summed(
            jnp.dot(pieces(taken), take_ref[n_col:, :], preferred_element_type=f32)
        )
        lines_in(r, 1, half).wait_recv()
        taken = by_cell(recv_ref[r, half:n_col, :])
        ghosts = ghosts + summed(
            jnp.dot(pieces(taken), take_ref[0:n_col, :], preferred_element_type=f32)
        )
        pairs = ghosts.reshape(4, 2, 8, FACES)
        pairs = pairs[:, 0] + pairs[:, 1]
        even = iota((4, 8, FACES), 1) % 2 == 0
        pairs = 0.25 * (pairs + jnp.where(even, pltpu.roll(pairs, 7, 1), pltpu.roll(pairs, 1, 1)))
        coarse = jnp.broadcast_to(pairs[:, None], (4, 2, 8, FACES)).reshape(64, FACES)
        ghosts = jnp.where(hanging, coarse, ghosts)

        sides = [ghosts[:, f * LANES : (f + 1) * LANES] for f in range(6)]
        inner_ref[0:64, :] += sides[0]
        inner_ref[448:512, :] += sides[1]
        for i in range(8):
            inner_ref[i * 64 : i * 64 + 8, :] += sides[2][i * 8 : i * 8 + 8]
            inner_ref[i * 64 + 56 : i * 64 + 64, :] += sides[3][i * 8 : i * 8 + 8]
        zbuf_ref[pl.ds(0, 64, stride=8), :] = sides[4]
        zbuf_ref[pl.ds(7, 64, stride=8), :] = sides[5]
        return (inner_ref[...] + zbuf_ref[...]) * scale

    def potential(v, lap):
        return v * v * v - v - gradient_energy * lap

    field_ref[...] = potential(conc_t_ref[...], laplacian(0))
    section = conc_t_ref[...] + time_step * laplacian(1)
    section_ref[...] = section
    field_ref[...] = section
    second = potential(section_ref[...], laplacian(2))
    field_ref[...] = second
    finished = 0.5 * (conc_t_ref[...] + section_ref[...] + time_step * laplacian(3))
    out_ref[0] = finished.T


def per_device(n_row, n_col):
    def run(conc, levels, neighbours, hanging, block_counts):
        blocks = conc.shape[0]
        vmem = pl.BlockSpec(memory_space=pltpu.VMEM)
        lines = n_col + SLAB
        whole = pltpu.VMEM((512, LANES), f32)

        def kernel(*refs):
            body(n_row, n_col, *refs)

        both = pl.pallas_call(
            kernel,
            out_shape=pltpu.VMEM((2, LANES, 512), f32),
            in_specs=[pl.BlockSpec(memory_space=pltpu.HBM)] * 5,
            out_specs=vmem,
            scratch_shapes=[
                pltpu.VMEM((blocks, 512), f32),
                pltpu.VMEM((LANES, 512), f32),
                pltpu.VMEM((1, blocks), jnp.int32),
                pltpu.VMEM((6, blocks), jnp.int32),
                pltpu.VMEM((6, blocks), jnp.int32),
                pltpu.VMEM((n_row, n_col), jnp.int32),
                pltpu.SemaphoreType.DMA((5,)),
                pltpu.VMEM((24, LANES), jnp.int32),
                pltpu.VMEM((n_row, n_col), f32),
                whole, whole, whole, whole, whole,
                pltpu.VMEM((2 * lines, FACES), bf16),
                pltpu.VMEM((2 * lines, FACES), bf16),
                pltpu.VMEM((FACES, LANES), bf16),
                pltpu.VMEM((ROUNDS, lines, LANES), f32),
                pltpu.VMEM((ROUNDS, lines, LANES), f32),
                pltpu.VMEM((n_col, LANES), f32),
                pltpu.SemaphoreType.DMA((ROUNDS,)),
                pltpu.SemaphoreType.DMA((ROUNDS, 2)),
                pltpu.SemaphoreType.DMA((ROUNDS, 2)),
                pltpu.SemaphoreType.DMA((ROUNDS, 2)),
                pltpu.SemaphoreType.DMA,
                pltpu.SemaphoreType.DMA,
                pltpu.SemaphoreType.REGULAR,
            ],
            compiler_params=pltpu.CompilerParams(
                collective_id=0, has_side_effects=True, vmem_limit_bytes=32 * 1024 * 1024
            ),
        )(
            *(
                pltpu.with_memory_space_constraint(v, pltpu.HBM)
                for v in (conc, levels.reshape(1, blocks), neighbours, hanging, block_counts.reshape(n_row, n_col))
            )
        )
        return both[0, :blocks], both[1, :blocks]

    return run


def solution(mesh):
    return jax.shard_map(
        per_device(mesh.shape["row"], mesh.shape["col"]),
        mesh=mesh,
        in_specs=(
            P(("row", "col"), None),
            P(("row", "col")),
            P(None, ("row", "col")),
            P(None, ("row", "col")),
            P(),
        ),
        out_specs=(P(("row", "col"), None), P(("row", "col"), None)),
        check_vma=False,
    )
```

```python
import jax
import jax.numpy as jnp
from jax import lax
from jax.experimental import pallas as pl
from jax.experimental.pallas import tpu as pltpu
from jax.sharding import PartitionSpec as P

MESH = pl.DeviceIdType.MESH
gradient_energy = 0.0625
time_step = 0.0004

LANES = 128
FACES = 6 * LANES
X_RING = 4
SLAB = 32
ROUNDS = 4
OUTER_FIRST = (2, 1, 3, 0)
BIG = 1e6
f32 = jnp.float32
bf16 = jnp.bfloat16


def iota(shape, dim):
    return lax.broadcasted_iota(jnp.int32, shape, dim)


def onehot(cond):
    return jnp.where(cond, 1.0, 0.0).astype(bf16)


def pieces(v):
    hi = v.astype(bf16)
    rest = v - hi.astype(f32)
    mid = rest.astype(bf16)
    lo = (rest - mid.astype(f32)).astype(bf16)
    return jnp.concatenate([hi, mid, lo], axis=0)


def turned(row):
    return jnp.broadcast_to(row, (LANES, LANES)).T


def layer_parts(ref):
    return [
        ref[0:64, :],
        ref[448:512, :],
        jnp.concatenate([ref[x * 64 : x * 64 + 8, :] for x in range(8)], axis=0),
        jnp.concatenate([ref[x * 64 + 56 : x * 64 + 64, :] for x in range(8)], axis=0),
        ref[pl.ds(0, 64, stride=8), :],
        ref[pl.ds(7, 64, stride=8), :],
    ]


def body(
    n_row, n_col,
    conc_ref, levels_ref, nb_ref, hang_ref, counts_ref,
    out_ref,
    give_t_ref, conc_in, pad_ref, levels_in, nb_in, hang_in, counts_in, load_sem,
    ints_ref, off_ref, field_ref, conc_t_ref, section_ref, inner_ref, zbuf_ref, give_ref, take_ref, local_ref,
    send_ref, recv_ref, mid_ref, send_sem, recv_sem, slab_send_sem, slab_recv_sem, mid_send_sem, mid_recv_sem, hello_sem,
):
    blocks = conc_ref.shape[0]
    z_ring = n_col // X_RING
    shift = z_ring // 4
    half = n_col // 2
    row = lax.axis_index("row")
    col = lax.axis_index("col")
    z = col // X_RING
    x = lax.rem(col, X_RING)
    below = lax.rem(row + n_row - 1, n_row)
    above = lax.rem(row + 1, n_row)

    def peer(dz, dx):
        return lax.rem(z + dz, z_ring) * X_RING + lax.rem(x + dx, X_RING)

    def line(dz, dx):
        return lax.rem(dz + shift, z_ring) * X_RING + dx

    own_line = shift * X_RING
    for r in range(ROUNDS):
        recv_ref[r, own_line : own_line + 1, :] = jnp.zeros((1, LANES), f32)

    barrier = pltpu.get_barrier_semaphore()

    def greet(dz, dx):
        pl.semaphore_signal(barrier, inc=1, device_id={"col": peer(dz, dx)}, device_id_type=MESH)

    def greet_pair(i, carry):
        greet(shift + 1 - i, 0)
        greet(z_ring - shift - 1 + i, 0)
        return carry

    lax.fori_loop(1, shift + 1, greet_pair, 0)
    for dx in range(1, X_RING):
        greet(0, dx)
    for other in (below, above):
        pl.semaphore_signal(barrier, inc=1, device_id={"row": other}, device_id_type=MESH)

    loads = [
        pltpu.make_async_copy(src, dst, load_sem.at[i])
        for i, (src, dst) in enumerate(
            (
                (counts_ref, counts_in),
                (nb_ref, nb_in),
                (conc_ref, conc_in),
                (hang_ref, hang_in),
                (levels_ref, levels_in),
            )
        )
    ]
    for load in loads:
        load.start()
    for load in loads:
        load.wait()

    counts = counts_in[...].astype(f32)
    before = onehot(iota((n_col, n_col), 0) < iota((n_col, n_col), 1))
    partial = jnp.dot(counts.astype(bf16), before, preferred_element_type=f32)
    totals = jnp.sum(counts, axis=1, keepdims=True)
    start = jnp.zeros((1, 1), f32)
    for r in range(n_row):
        off_ref[r : r + 1, :] = partial[r : r + 1, :] + start
        start = start + totals[r : r + 1, :]
    lane = iota((1, LANES), 1)
    mine = lane == col

    def pick(v):
        return jnp.sum(jnp.where(mine, v, 0.0), axis=1, keepdims=True)

    def ranges(r):
        offsets = off_ref[pl.ds(r, 1), :]
        held = counts_in[pl.ds(r, 1), :].astype(f32)
        return offsets, held

    off_row, held_row = ranges(row)
    off_low, held_low = (pick(v) for v in ranges(below))
    off_high, held_high = (pick(v) for v in ranges(above))
    my_count = pick(held_row)
    row_start = off_row[:, 0:1]
    row_end = row_start + jnp.sum(held_row, axis=1, keepdims=True)
    off_turned = turned(off_row)

    pad_ref[0:blocks, :] = conc_in[...]
    pad_ref[blocks:, :] = jnp.zeros((LANES - blocks, 512), f32)
    live_rows = iota((LANES, 512), 0).astype(f32) < my_count
    start_field = jnp.where(live_rows, pad_ref[...], 0.0).T
    field_ref[...] = start_field
    conc_t_ref[...] = start_field

    ints_ref[0:8, :] = jnp.full((8, LANES), -1, jnp.int32)
    ints_ref[8:24, :] = jnp.zeros((16, LANES), jnp.int32)
    ints_ref[0:6, 0:blocks] = nb_in[...]
    ints_ref[8:14, 0:blocks] = hang_in[...]
    ints_ref[16:17, 0:blocks] = levels_in[...]
    level = ints_ref[16:17, :]
    scale = jnp.where(level == 0, 1.0, jnp.where(level == 1, 4.0, jnp.where(level == 2, 16.0, 0.0)))
    hanging = jnp.concatenate([ints_ref[8 + f : 9 + f, :] for f in range(6)], axis=1) > 0

    partner_parts, give_parts, take_parts, slab_give, slab_take, low_parts, high_parts = [], [], [], [], [], [], []
    for f in range(6):
        target = ints_ref[f : f + 1, :].astype(f32)
        live = (target >= 0.0) & (lane.astype(f32) < my_count)
        in_row = live & (target >= row_start) & (target < row_end)
        reached = off_turned <= target
        owner = jnp.sum(jnp.where(reached, 1.0, 0.0), axis=0, keepdims=True).astype(jnp.int32) - 1
        first = jnp.max(jnp.where(reached, off_turned, 0.0), axis=0, keepdims=True)
        here = in_row & (owner == col)
        far = in_row & (owner != col)
        low = live & (target >= off_low) & (target < off_low + held_low)
        high = live & (target >= off_high) & (target < off_high + held_high)
        slot = jnp.where(in_row, target - first, jnp.where(low, target - off_low, target - off_high))
        apart = (((owner >> 2) - z + shift) & (z_ring - 1)) * X_RING + ((owner - x) & (X_RING - 1))
        partner_parts.append(jnp.where(far, apart, -1))
        give_key = (lane + f * LANES).astype(f32)
        take_key = slot + float((f ^ 1) * LANES)
        give_parts.append(give_key)
        take_parts.append(take_key)
        slab_give.append(jnp.where(low, give_key, jnp.where(high, give_key + 1024.0, BIG)))
        slab_take.append(jnp.where(low, take_key, jnp.where(high, take_key + 1024.0, BIG)))
        low_parts.append(jnp.where(low, 1.0, 0.0))
        high_parts.append(jnp.where(high, 1.0, 0.0))
        local_ref[f * LANES : (f + 1) * LANES, :] = onehot(
            (iota((LANES, LANES), 0).astype(f32) == slot) & here
        )
    partner = jnp.concatenate(partner_parts, axis=1)
    low_all = jnp.concatenate(low_parts, axis=1)
    high_all = jnp.concatenate(high_parts, axis=1)
    matched = iota((n_col, FACES), 0) == partner
    slab_line = iota((SLAB, FACES), 0)
    slab_id = (slab_line + jnp.where(slab_line >= SLAB // 2, SLAB // 2, 0)).astype(f32)
    n_low = jnp.sum(low_all, axis=1, keepdims=True)
    for ref, keys, slab_keys in ((give_ref, give_parts, slab_give), (take_ref, take_parts, slab_take)):
        key = jnp.concatenate(keys, axis=1)
        least = jnp.min(jnp.where(matched, key, BIG), axis=1, keepdims=True)
        for i, lines in enumerate((onehot(matched & (key == least)), onehot(matched & (key != least)))):
            ref[i * half : (i + 1) * half, :] = lines[half:]
            ref[n_col + i * half : n_col + (i + 1) * half, :] = lines[:half]
        slab_key = jnp.concatenate(slab_keys, axis=1)
        smaller = jnp.zeros((1, FACES), f32)
        for f in range(6):
            smaller = smaller + jnp.sum(
                jnp.where(turned(slab_keys[f])[:, 0:1] < slab_key, 1.0, 0.0), axis=0, keepdims=True
            )
        place = jnp.where(low_all > 0.0, smaller, jnp.where(high_all > 0.0, smaller - n_low + SLAB, -1.0))
        ref[2 * n_col : 2 * n_col + SLAB, :] = onehot(slab_id == place)
        ref[2 * n_col + SLAB : 2 * n_col + 2 * SLAB, :] = onehot(slab_id + SLAB // 2 == place)
    zbuf_ref[...] = jnp.zeros((512, LANES), f32)
    give_t_ref[...] = give_ref[0:n_col, :].astype(f32).T.astype(bf16)


    def start_copy(r, dz, dx, far, left=None):
        pltpu.make_async_remote_copy(
            src_ref=(send_ref.at[r] if left is None else mid_ref).at[pl.ds(line(dz, dx), 1)],
            dst_ref=recv_ref.at[r, pl.ds(line(z_ring - dz, lax.rem(X_RING - dx, X_RING)), 1)],
            send_sem=send_sem.at[r],
            recv_sem=recv_sem.at[r, far],
            device_id={"col": peer(dz if left is None else left, dx)},
            device_id_type=MESH,
        ).start()

    def bundle(dz):
        lines = pl.ds(line(2 * dz, 0), 2 * X_RING)
        return pltpu.make_async_remote_copy(
            src_ref=send_ref.at[0, lines],
            dst_ref=mid_ref.at[lines],
            send_sem=mid_send_sem,
            recv_sem=mid_recv_sem,
            device_id={"col": peer(dz, 0)},
            device_id_type=MESH,
        )

    def bundles_in():
        lines = pl.ds(0, (z_ring // 2 - 1) * 2 * X_RING)
        return pltpu.make_async_remote_copy(
            src_ref=send_ref.at[0, lines],
            dst_ref=mid_ref.at[lines],
            send_sem=mid_send_sem,
            recv_sem=mid_recv_sem,
            device_id={"col": peer(1, 0)},
            device_id_type=MESH,
        )

    def relay():
        pl.semaphore_wait(barrier, 2 * shift + X_RING - 1 + 2)
        bundle(z_ring - shift).start()
        pl.semaphore_signal(hello_sem, inc=1, device_id={"col": peer(shift, 0)}, device_id_type=MESH)

        def first_leg(i, carry):
            bundle(shift - i).start()
            bundle(z_ring - shift + i).start()
            return carry

        lax.fori_loop(1, shift, first_leg, 0)
        slabs = [slab_copy(0, 0, below), slab_copy(0, 1, above)]
        for copy in slabs:
            copy.start()
        pl.semaphore_wait(hello_sem, 1)
        bundles_in().wait_recv()
        for dx in OUTER_FIRST:
            start_copy(0, z_ring // 2, dx, 1, z_ring - shift)

        def second_leg(far):
            def step(i, carry):
                away = z_ring // 2 - i
                for dx in OUTER_FIRST:
                    start_copy(0, away, dx, far, (away + 1) // 2)
                    start_copy(0, z_ring - away, dx, far, lax.rem(z_ring - away // 2, z_ring))
                return carry

            return step

        lax.fori_loop(1, z_ring // 2 - shift, second_leg(1), 0)
        for dx in OUTER_FIRST:
            start_copy(0, shift, dx, 0, shift // 2)
            start_copy(0, z_ring - shift, dx, 1, z_ring - shift // 2)
        lax.fori_loop(z_ring // 2 - shift + 1, z_ring // 2 - 1, second_leg(0), 0)
        for dz in (1, z_ring - 1, 0):
            for dx in OUTER_FIRST:
                if dz or dx:
                    start_copy(0, dz, dx, 0)
        return slabs

    def slab_copy(r, side, other):
        part = SLAB // 2
        return pltpu.make_async_remote_copy(
            src_ref=send_ref.at[r, pl.ds(n_col + side * part, part)],
            dst_ref=recv_ref.at[r, pl.ds(n_col + (1 - side) * part, part)],
            send_sem=slab_send_sem.at[r, side],
            recv_sem=slab_recv_sem.at[r, side],
            device_id={"row": other},
            device_id_type=MESH,
        )

    def lines_in(r, far, count):
        return pltpu.make_async_remote_copy(
            src_ref=send_ref.at[r, pl.ds(0, count)],
            dst_ref=recv_ref.at[r, pl.ds(0, count)],
            send_sem=send_sem.at[r],
            recv_sem=recv_sem.at[r, far],
            device_id={"col": peer(1, 0)},
            device_id_type=MESH,
        )

    def summed(v):
        return v[0:64] + (v[64:128] + v[128:192])

    def by_cell(lines):
        return jnp.concatenate([lines[:, 0:64], lines[:, 64:128]], axis=0).T

    def laplacian(r):
        layers = layer_parts(field_ref)
        cut = pieces(jnp.concatenate(layers, axis=1))

        def give(first, last):
            if first:
                given = lax.dot_general(
                    give_ref[first:last, :], cut, (((1,), (1,)), ((), ())), preferred_element_type=f32
                )
                return given[:, 0:64] + (given[:, 64:128] + given[:, 128:192])
            given = summed(jnp.dot(cut, give_t_ref[...], preferred_element_type=f32))
            return jnp.concatenate([given[:, 0:half], given[:, half:n_col]], axis=0).T

        def outward(far):
            def step(away, carry):
                for dx in OUTER_FIRST:
                    start_copy(r, away, dx, far)
                    start_copy(r, z_ring - away, dx, far)
                return carry

            return lambda i, carry: step(z_ring // 2 - i, carry)

        given = give(0, n_col)
        send_ref[r, half:n_col, :] = given
        if r > 0:
            for dx in OUTER_FIRST:
                start_copy(r, z_ring // 2, dx, 1)
            lax.fori_loop(1, z_ring // 2 - shift, outward(1), 0)
            for dx in OUTER_FIRST:
                start_copy(r, shift, dx, 0)
        given = give(n_col, 2 * n_col + 2 * SLAB)
        send_ref[r, 0:half, 0:64] = given[0:half]
        send_ref[r, 0:half, 64:128] = given[half:n_col]
        send_ref[r, n_col:, 0:64] = given[n_col : n_col + SLAB]
        send_ref[r, n_col:, 64:128] = given[n_col + SLAB :]
        if r > 0:
            for dx in OUTER_FIRST:
                start_copy(r, z_ring - shift, dx, 1)
            lax.fori_loop(z_ring // 2 - shift + 1, z_ring // 2, outward(0), 0)
            for dx in range(1, X_RING):
                start_copy(r, 0, dx, 0)
            slabs = [slab_copy(r, 0, below), slab_copy(r, 1, above)]
            for copy in slabs:
                copy.start()
        else:
            slabs = relay()

        cells = field_ref[...]
        cube = cells.reshape(8, 8, 8, LANES)
        zero_x = jnp.zeros((1, 8, 8, LANES), f32)
        zero_y = jnp.zeros((8, 1, 8, LANES), f32)
        steps = jnp.concatenate([zero_x, cube[:7]], axis=0) + jnp.concatenate([cube[1:], zero_x], axis=0)
        steps = steps + jnp.concatenate([zero_y, cube[:, :7]], axis=1)
        steps = steps + jnp.concatenate([cube[:, 1:], zero_y], axis=1)
        columns = cells.reshape(64, 8, LANES)
        z_at = iota((64, 8, LANES), 1)
        prev_z = jnp.where(z_at > 0, pltpu.roll(columns, 1, 1), 0.0)
        next_z = jnp.where(z_at < 7, pltpu.roll(columns, 7, 1), 0.0)
        inner_ref[...] = steps.reshape(512, LANES) + (prev_z + next_z).reshape(512, LANES) - 6.0 * cells
        near_ghosts = []
        for f in range(6):
            g = f ^ 1
            part = jnp.dot(
                cut[:, g * LANES : (g + 1) * LANES],
                local_ref[f * LANES : (f + 1) * LANES, :],
                preferred_element_type=f32,
            )
            near_ghosts.append(summed(part))
        ghosts = jnp.concatenate(near_ghosts, axis=1)

        if r == ROUNDS - 1:
            out_ref[1] = cells.T
            bundles_in().wait_send()
            for done in range(ROUNDS):
                lines_in(done, 0, n_col - 1).wait_send()
                slab_copy(done, 0, below).wait_send()
                slab_copy(done, 1, above).wait_send()

        lines_in(r, 0, half - 1).wait_recv()
        for copy in slabs:
            copy.wait_recv()
        taken = jnp.concatenate([by_cell(recv_ref[r, 0:half, :]), by_cell(recv_ref[r, n_col:, :])], axis=1)
        ghosts = ghosts + summed(
            jnp.dot(pieces(taken), take_ref[n_col:, :], preferred_element_type=f32)
        )
        lines_in(r, 1, half).wait_recv()
        taken = by_cell(recv_ref[r, half:n_col, :])
        ghosts = ghosts + summed(
            jnp.dot(pieces(taken), take_ref[0:n_col, :], preferred_element_type=f32)
        )
        pairs = ghosts.reshape(4, 2, 8, FACES)
        pairs = pairs[:, 0] + pairs[:, 1]
        even = iota((4, 8, FACES), 1) % 2 == 0
        pairs = 0.25 * (pairs + jnp.where(even, pltpu.roll(pairs, 7, 1), pltpu.roll(pairs, 1, 1)))
        coarse = jnp.broadcast_to(pairs[:, None], (4, 2, 8, FACES)).reshape(64, FACES)
        ghosts = jnp.where(hanging, coarse, ghosts)

        sides = [ghosts[:, f * LANES : (f + 1) * LANES] for f in range(6)]
        inner_ref[0:64, :] += sides[0]
        inner_ref[448:512, :] += sides[1]
        for i in range(8):
            inner_ref[i * 64 : i * 64 + 8, :] += sides[2][i * 8 : i * 8 + 8]
            inner_ref[i * 64 + 56 : i * 64 + 64, :] += sides[3][i * 8 : i * 8 + 8]
        zbuf_ref[pl.ds(0, 64, stride=8), :] = sides[4]
        zbuf_ref[pl.ds(7, 64, stride=8), :] = sides[5]
        return (inner_ref[...] + zbuf_ref[...]) * scale

    def potential(v, lap):
        return v * v * v - v - gradient_energy * lap

    field_ref[...] = potential(conc_t_ref[...], laplacian(0))
    section = conc_t_ref[...] + time_step * laplacian(1)
    section_ref[...] = section
    field_ref[...] = section
    second = potential(section_ref[...], laplacian(2))
    field_ref[...] = second
    finished = 0.5 * (conc_t_ref[...] + section_ref[...] + time_step * laplacian(3))
    out_ref[0] = finished.T


def per_device(n_row, n_col):
    def run(conc, levels, neighbours, hanging, block_counts):
        blocks = conc.shape[0]
        vmem = pl.BlockSpec(memory_space=pltpu.VMEM)
        lines = n_col + SLAB
        whole = pltpu.VMEM((512, LANES), f32)

        def kernel(*refs):
            body(n_row, n_col, *refs)

        both = pl.pallas_call(
            kernel,
            out_shape=pltpu.VMEM((2, LANES, 512), f32),
            in_specs=[pl.BlockSpec(memory_space=pltpu.HBM)] * 5,
            out_specs=vmem,
            scratch_shapes=[
                pltpu.VMEM((FACES, n_col), bf16),
                pltpu.VMEM((blocks, 512), f32),
                pltpu.VMEM((LANES, 512), f32),
                pltpu.VMEM((1, blocks), jnp.int32),
                pltpu.VMEM((6, blocks), jnp.int32),
                pltpu.VMEM((6, blocks), jnp.int32),
                pltpu.VMEM((n_row, n_col), jnp.int32),
                pltpu.SemaphoreType.DMA((5,)),
                pltpu.VMEM((24, LANES), jnp.int32),
                pltpu.VMEM((n_row, n_col), f32),
                whole, whole, whole, whole, whole,
                pltpu.VMEM((2 * lines, FACES), bf16),
                pltpu.VMEM((2 * lines, FACES), bf16),
                pltpu.VMEM((FACES, LANES), bf16),
                pltpu.VMEM((ROUNDS, lines, LANES), f32),
                pltpu.VMEM((ROUNDS, lines, LANES), f32),
                pltpu.VMEM((n_col, LANES), f32),
                pltpu.SemaphoreType.DMA((ROUNDS,)),
                pltpu.SemaphoreType.DMA((ROUNDS, 2)),
                pltpu.SemaphoreType.DMA((ROUNDS, 2)),
                pltpu.SemaphoreType.DMA((ROUNDS, 2)),
                pltpu.SemaphoreType.DMA,
                pltpu.SemaphoreType.DMA,
                pltpu.SemaphoreType.REGULAR,
            ],
            compiler_params=pltpu.CompilerParams(
                collective_id=0, has_side_effects=True, vmem_limit_bytes=32 * 1024 * 1024
            ),
        )(
            *(
                pltpu.with_memory_space_constraint(v, pltpu.HBM)
                for v in (conc, levels.reshape(1, blocks), neighbours, hanging, block_counts.reshape(n_row, n_col))
            )
        )
        return both[0, :blocks], both[1, :blocks]

    return run


def solution(mesh):
    return jax.shard_map(
        per_device(mesh.shape["row"], mesh.shape["col"]),
        mesh=mesh,
        in_specs=(
            P(("row", "col"), None),
            P(("row", "col")),
            P(None, ("row", "col")),
            P(None, ("row", "col")),
            P(),
        ),
        out_specs=(P(("row", "col"), None), P(("row", "col"), None)),
        check_vma=False,
    )
```
